128 devices in a mesh: island: 8 (over z, core), seq: 16 (over y, x).
Axes of the slice: x: 4, y: 4, z: 4, core: 2. Of those that a mesh axis runs over, the one named last changes fastest.
Arguments:
- query: bfloat16 [32768, 2560], P(('island', 'seq')), parts along dimension 0, may hold values from -6 to 6
- key: bfloat16 [32768, 512], P(('island', 'seq')), parts along dimension 0, may hold values from -6 to 6
- value: bfloat16 [32768, 512], P(('island', 'seq')), parts along dimension 0, may hold values from -6 to 6
- attn_out: bfloat16 [32768, 2560], P(('island', 'seq')), parts along dimension 0, may hold values from -6 to 6
- out_grad: bfloat16 [32768, 2560], P(('island', 'seq')), parts along dimension 0, may hold values from -6 to 6
- log_sums: float32 [20, 32768], P(None, ('island', 'seq')), parts along dimension 1, may hold values from 5 to 8
- block_order: int32 [256], P('island'), parts along dimension 0, may hold values from 0 to 31, each once
- doc_lengths: int32 [32], P('island'), parts along dimension 0, may hold values from 1 to 2048, 4096 in all
Outputs:
- query_grad: bfloat16 [32768, 2560], P(('island', 'seq')), parts along dimension 0
- key_grad: bfloat16 [32768, 512], P(('island', 'seq')), parts along dimension 0
- value_grad: bfloat16 [32768, 512], P(('island', 'seq')), parts along dimension 0
The draws below stay inside these ranges and needn't reach their ends.
There are 8 independent parts, one for each index of `island`. The reference program is written for one: setup_inputs(seed, part) draws one part's arguments, and reference() takes and returns one part's arrays. A program takes and returns all parts, laid end to end along the dimension named above; each array names one. Nothing has to cross between parts.
Inputs may be any that keep to these rules, and one draw needn't show every extreme that they name: `block_order`: every number appears once. `doc_lengths`: the lengths sum to 4096 and the largest is exactly 2048.
All inputs are finite; a program needn't handle non-finite values.
Results may differ from the reference program's by a relative error of at most 0.006.
Values may be sent and summed in bfloat16 or wider, within the bound.
A program may use at most 128 MiB of HBM per device.

```python
import math
import jax
import jax.numpy as jnp
import numpy as np
from jax import lax

HQ = 20
KVH = 4
HD = 128
BLK = 128
DOCS = 4
TOK_DEV = 256
TOKENS = 4096
NBLK = 32
MOST = 2048


def shard_levels(stream_key, extent, cuts, least, high):
    def one(dim, blocks):
        steps = jax.random.uniform(jax.random.fold_in(jax.random.fold_in(stream_key, 6), dim), (blocks,), jnp.float32, least / len(cuts), high / len(cuts))
        return jnp.repeat(jnp.exp(steps), extent[dim] // blocks).reshape((-1,) + (1,) * (len(extent) - dim - 1))

    level = one(*cuts[0])
    for cut in cuts[1:]:
        level = level * one(*cut)
    return level


def length_profile(amount, total, reach, lean):
    portions = [(1 << 20) // math.isqrt(rank ** lean) + 1 for rank in range(2, amount + 1)]
    surplus, holding = total - reach - (amount - 1), [1] * (amount - 1)
    while surplus > 0:
        candidates = [i for i in range(amount - 1) if holding[i] < reach]
        pool, remaining = sum([portions[i] for i in candidates]), surplus
        for i in candidates:
            extra = min(reach - holding[i], max(1, remaining * portions[i] // pool), surplus)
            holding[i] = holding[i] + extra
            surplus = surplus - extra
    return np.array([reach] + holding)


def ragged(rng, count, total, bound, skew):
    if count == 2:
        one = jax.random.randint(rng, (), max(1, total - bound), min(bound, total - 1) + 1)
        return jnp.stack([one, total - one])
    tallies = jnp.asarray(length_profile(count, total, bound, skew), jnp.int32)
    pairs = (count - 1) // 2
    donor, taker = tallies[1:1 + 2 * pairs:2], tallies[2:2 + 2 * pairs:2]
    margin = jnp.minimum(donor - 1, bound - taker)
    shifted = jax.random.randint(jax.random.fold_in(rng, 1), (pairs,), 0, 1 << 20) % (margin + 1)
    tallies = tallies.at[1:1 + 2 * pairs:2].set(donor - shifted).at[2:2 + 2 * pairs:2].set(taker + shifted)
    return tallies[jax.random.permutation(jax.random.fold_in(rng, 2), count)]


def scatter_about(rng, shape, scale, limit, shards=(), kind=jnp.bfloat16):
    factor_of = shard_levels(rng, shape, shards, -0.22, 0.18) if shards else 1.0
    array = jax.random.normal(rng, shape, jnp.float32) * scale * factor_of
    return jnp.minimum(jnp.maximum(array, -limit), limit).astype(kind)


def setup_inputs(seed: int = 0, part: int = 0) -> dict:
    keys = jax.random.split(jax.random.key(seed), 9)
    part_splits = jax.random.split(jax.random.fold_in(keys[8], part), 9)
    query = scatter_about(part_splits[0], (TOKENS, HQ * HD), 1.0, 6.0, ((0, 16),))
    key = scatter_about(part_splits[1], (TOKENS, KVH * HD), 1.0, 6.0, ((0, 16),))
    value = scatter_about(part_splits[2], (TOKENS, KVH * HD), 1.0, 6.0, ((0, 16),))
    attn_out = scatter_about(part_splits[3], (TOKENS, HQ * HD), 1.0, 6.0, ((0, 16),))
    out_grad = scatter_about(part_splits[4], (TOKENS, HQ * HD), 1.0, 6.0, ((0, 16),))
    log_sums = jnp.clip(5.0 + 3.0 * jax.random.uniform(part_splits[5], (HQ, TOKENS), jnp.float32) ** shard_levels(part_splits[5], (HQ, TOKENS), ((1, 16),), -0.2, 0.2), 5.0, 8.0)
    block_order = jax.random.permutation(part_splits[6], NBLK).astype(jnp.int32)
    doc_lengths = ragged(part_splits[7], DOCS, TOKENS, MOST, 2).astype(jnp.int32)
    return {"query": query, "key": key, "value": value, "attn_out": attn_out, "out_grad": out_grad, "log_sums": log_sums, "block_order": block_order, "doc_lengths": doc_lengths}


def layout(block_order, doc_lengths):
    count = block_order.shape[0]
    offsets = jnp.tile(jnp.arange(BLK, dtype=jnp.int32), count)
    seq_pos = (jnp.repeat(block_order, BLK) * BLK + offsets).astype(jnp.int32)
    ends = jnp.cumsum(doc_lengths).astype(jnp.int32)
    doc_ids = lax.optimization_barrier(jnp.sum((ends[None, :] <= seq_pos[:, None]).astype(jnp.int32), axis=1)).astype(jnp.int32)
    return (seq_pos, doc_ids)

def reference(query, key, value, attn_out, out_grad, log_sums, block_order, doc_lengths):
    scale = 1.0 / math.sqrt(HD)
    seq_pos, doc_ids = layout(block_order, doc_lengths)
    rows = TOK_DEV
    blocks = TOKENS // rows
    group = HQ // KVH
    key_heads = key.astype(jnp.float32).reshape(TOKENS, KVH, HD)
    value_heads = value.astype(jnp.float32).reshape(TOKENS, KVH, HD)

    def one_block(carry, number):
        key_acc, value_acc = carry
        begin = (number * rows).astype(jnp.int32)
        queries = lax.dynamic_slice_in_dim(query, begin, rows, 0).astype(jnp.float32).reshape(rows, KVH, group, HD)
        grads_out = lax.dynamic_slice_in_dim(out_grad, begin, rows, 0).astype(jnp.float32).reshape(rows, KVH, group, HD)
        outputs = lax.dynamic_slice_in_dim(attn_out, begin, rows, 0).astype(jnp.float32).reshape(rows, KVH, group, HD)
        sums = lax.dynamic_slice_in_dim(log_sums, begin, rows, 1).reshape(KVH, group, rows)
        delta = lax.optimization_barrier(jnp.sum(grads_out * outputs, axis=3)).transpose(1, 2, 0)
        query_pos = lax.dynamic_slice_in_dim(seq_pos, begin, rows, 0)
        query_doc = lax.dynamic_slice_in_dim(doc_ids, begin, rows, 0)
        allowed = (query_doc[:, None] == doc_ids[None, :]) & (seq_pos[None, :] <= query_pos[:, None])
        scores = jnp.einsum('rgjd,kgd->gjrk', queries, key_heads) * scale
        probs = jnp.where(allowed, jnp.exp(scores - sums[..., None]), 0.0)
        dprobs = jnp.einsum('rgjd,kgd->gjrk', grads_out, value_heads)
        dscores = lax.optimization_barrier((probs * (dprobs - delta[..., None])).astype(jnp.bfloat16)).astype(jnp.float32)
        probs_low = lax.optimization_barrier(probs.astype(jnp.bfloat16)).astype(jnp.float32)
        query_part = jnp.einsum('gjrk,kgd->rgjd', dscores, key_heads).reshape(rows, HQ * HD) * scale
        key_acc = key_acc + jnp.einsum('gjrk,rgjd->kgd', dscores, queries).reshape(TOKENS, KVH * HD) * scale
        value_acc = value_acc + jnp.einsum('gjrk,rgjd->kgd', probs_low, grads_out).reshape(TOKENS, KVH * HD)
        return ((key_acc, value_acc), query_part.astype(jnp.bfloat16))
    empty = jnp.zeros((TOKENS, KVH * HD), jnp.float32)
    (key_acc, value_acc), pieces = lax.scan(one_block, (empty, empty), jnp.arange(blocks, dtype=jnp.int32))
    return (pieces.reshape(TOKENS, HQ * HD), key_acc.astype(jnp.bfloat16), value_acc.astype(jnp.bfloat16))
```

```python
import functools
import math

import jax
import jax.numpy as jnp
from jax import lax
from jax.experimental import pallas as pl
from jax.experimental.pallas import tpu as pltpu
from jax.sharding import PartitionSpec as P

MESH = pl.DeviceIdType.MESH
HD = 128
BLK = 128
SIDE = 4
ROWS = 256
GROUP = 5
QW = GROUP * HD
TOKENS = 4096
NBLK = 32
STEP = 256
PAD = STEP - BLK
SCALE = 1.0 / math.sqrt(HD)
LOG2E = math.log2(math.e)
NT = (((1,), (1,)), ((), ()))
TN = (((0,), (0,)), ((), ()))


def place():
    core = lax.rem(lax.axis_index("island"), 2)
    seq = lax.axis_index("seq")
    x, y = lax.rem(seq, SIDE), seq // SIDE
    a = x + core * (y - x)
    b = y + core * (x - y)
    return a, b, 1 + 3 * core, SIDE - 3 * core


class Wires:
    def __init__(self, send_sems, recv_sems):
        self.send_sems, self.recv_sems, self.count = send_sems, recv_sems, 0

    def send(self, src, dst, device):
        n = self.count
        self.count += 1
        copy = pltpu.make_async_remote_copy(
            src, dst, self.send_sems.at[n], self.recv_sems.at[n], device_id=device, device_id_type=MESH
        )
        copy.start()
        return copy


def span(start, size):
    return pl.ds(pl.multiple_of(start * size, size), size)


def greet(devices):
    barrier = pltpu.get_barrier_semaphore()
    for device in devices:
        pl.semaphore_signal(barrier, inc=1, device_id=device, device_id_type=MESH)
    pl.semaphore_wait(barrier, len(devices))


def gather_kernel(
    q_ref, k_ref, v_ref, o_ref, do_ref, lse_ref, qx, dox, kv, auxx, o_buf, do_buf, aux, ssem, rsem, lsem
):
    a, b, sa, sb = place()
    A = [lax.rem(a + t, SIDE) for t in range(SIDE)]
    B = [lax.rem(b + t, SIDE) for t in range(SIDE)]

    def dev(aa, bb):
        return {"seq": aa * sa + bb * sb}

    def slot(aa, bb):
        return span(aa * sa + bb * sb, ROWS)

    loads = [
        pltpu.make_async_copy(o_ref, o_buf, lsem.at[0]),
        pltpu.make_async_copy(do_ref, do_buf, lsem.at[1]),
    ]
    for load in loads:
        load.start()
    greet([dev(A[1], b), dev(A[3], b), dev(A[2], b), dev(a, B[1]), dev(a, B[3])])
    wires = Wires(ssem, rsem)
    mine = slot(a, b)
    first = {}
    for t in (1, 3, 2):
        first[t] = [
            wires.send(s.at[:, span(A[t], HD)], kv.at[mine, pl.ds(n * HD, HD)], dev(A[t], b))
            for n, s in enumerate((k_ref, v_ref))
        ]
    local = [
        pltpu.make_async_copy(k_ref.at[:, span(a, HD)], kv.at[mine, pl.ds(0, HD)], lsem.at[2]),
        pltpu.make_async_copy(v_ref.at[:, span(a, HD)], kv.at[mine, pl.ds(HD, HD)], lsem.at[3]),
        pltpu.make_async_copy(q_ref.at[:, span(a, QW)], qx.at[span(a, ROWS)], lsem.at[4]),
        pltpu.make_async_copy(do_ref.at[:, span(a, QW)], dox.at[span(a, ROWS)], lsem.at[5]),
    ]
    for copy in local:
        copy.start()
    rest = []
    for t in (1, 3, 2):
        for s, d in ((q_ref, qx), (do_ref, dox)):
            rest.append(wires.send(s.at[:, span(A[t], QW)], d.at[span(a, ROWS)], dev(A[t], b)))

    passed = {}

    def spread(t):
        rows = slot(A[t], b)
        passed[t] = (
            wires.send(kv.at[rows], kv.at[rows], dev(a, B[1])),
            wires.send(kv.at[rows], kv.at[rows], dev(a, B[3])),
        )

    local[0].wait()
    local[1].wait()
    spread(0)
    for t in (1, 3, 2):
        for copy in first[SIDE - t]:
            copy.wait_recv()
        spread(t)

    for load in loads:
        load.wait()
    ones = jnp.ones((8, HD), jnp.bfloat16)
    aux[...] = jnp.zeros_like(aux)
    for g in range(SIDE):
        for h in range(GROUP):
            n = g * GROUP + h
            cols = slice(n * HD, (n + 1) * HD)
            prod = o_buf[:, cols].astype(jnp.float32) * do_buf[:, cols].astype(jnp.float32)
            high = prod.astype(jnp.bfloat16)
            low = (prod - high.astype(jnp.float32)).astype(jnp.bfloat16)
            delta = lax.dot_general(ones, high, NT, preferred_element_type=jnp.float32)
            delta += lax.dot_general(ones, low, NT, preferred_element_type=jnp.float32)
            aux[g, h : h + 1, :] = lse_ref[n : n + 1, :] * LOG2E
            aux[g, 8 + h : 9 + h, :] = delta[0:1]
    for t in (1, 3, 2):
        rest.append(wires.send(aux.at[A[t]], auxx.at[a], dev(A[t], b)))
    own = pltpu.make_async_copy(aux.at[a], auxx.at[a], lsem.at[6])
    own.start()

    second = []
    for t in (0, 1, 3, 2):
        up, down = passed[t]
        up.wait_recv()
        if t in (0, 1):
            rows = slot(A[t], B[3])
            second.append(wires.send(kv.at[rows], kv.at[rows], dev(a, B[1])))
        down.wait_recv()
        if t in (2, 3):
            rows = slot(A[t], B[1])
            second.append(wires.send(kv.at[rows], kv.at[rows], dev(a, B[3])))
    for copy in rest + second:
        copy.wait()
    for t in (1, 3, 2):
        for copy in first[t]:
            copy.wait_send()
    for t in range(SIDE):
        for copy in passed[t]:
            copy.wait_send()
    for copy in local[2:] + [own]:
        copy.wait()


def attend_kernel(
    order, docs, qx, dox, aux, kv, dq_ref, dkv_ref, keys, acc, qs, dos, dqt, inverse, sems
):
    a, b, sa, sb = place()

    def invert(n, carry):
        inverse[order[n]] = n
        return carry

    lax.fori_loop(0, NBLK, invert, 0)

    def load(c):
        return pltpu.make_async_copy(
            kv.at[span(inverse[c], BLK)], keys.at[pl.ds(pl.multiple_of(PAD + c * BLK, BLK), BLK)], sems.at[c]
        )

    def start(c, carry):
        load(c).start()
        return carry

    lax.fori_loop(0, NBLK, start, 0)
    keys[0:PAD, :] = jnp.zeros((PAD, 2 * HD), jnp.bfloat16)
    acc[...] = jnp.zeros_like(acc)
    e0 = docs[0]
    e1 = e0 + docs[1]
    e2 = e1 + docs[2]

    def finish(c, carry):
        load(c).wait()
        return carry

    lax.fori_loop(0, NBLK, finish, 0)

    def block(i, carry):
        aa = i // 2
        j = order[(aa * sa + b * sb) * 2 + lax.rem(i, 2)]
        rows = span(i, BLK)
        for h in range(GROUP):
            part = pl.ds(h * BLK, BLK)
            qs[part, :] = qx[rows, h * HD : (h + 1) * HD]
            dos[part, :] = dox[rows, h * HD : (h + 1) * HD]
        tok = pl.ds(pl.multiple_of(lax.rem(i, 2) * BLK, BLK), BLK)
        lse = jnp.concatenate([aux[aa, h : h + 1, tok] for h in range(GROUP)], axis=1)
        delta = jnp.concatenate([aux[aa, 8 + h : 9 + h, tok] for h in range(GROUP)], axis=1)
        pos = j * BLK + lax.broadcasted_iota(jnp.int32, (1, BLK), 1)
        begin = jnp.zeros((1, BLK), jnp.int32)
        low = jnp.int32(0)
        for e in (e0, e1, e2):
            begin = jnp.where(pos >= e, e, begin)
            low = jnp.where(j * BLK >= e, e, low)
        low = low // BLK
        dqt[...] = jnp.zeros_like(dqt)
        steps = (j - low + 1 + STEP // BLK - 1) // (STEP // BLK)

        def step(s, carry2):
            top = j - s * (STEP // BLK)
            at = pl.ds(pl.multiple_of(top * BLK, BLK), STEP)
            k = keys[at, 0:HD]
            v = keys[at, HD : 2 * HD]
            where = top * BLK - PAD + lax.broadcasted_iota(jnp.int32, (STEP, BLK), 0)
            allowed = (where >= begin) & (where <= pos)
            st = lax.dot_general(k, qs[...], NT, preferred_element_type=jnp.float32)
            dpt = lax.dot_general(v, dos[...], NT, preferred_element_type=jnp.float32)
            p_parts, d_parts = [], []
            for h in range(GROUP):
                part = slice(h * BLK, (h + 1) * BLK)
                p = jnp.exp2(st[:, part] * (SCALE * LOG2E) - lse[:, part])
                p = jnp.where(allowed, p, 0.0)
                d = p * (dpt[:, part] - delta[:, part])
                p_parts.append(p.astype(jnp.bfloat16))
                d_parts.append(d.astype(jnp.bfloat16))
            pt = jnp.concatenate(p_parts, axis=1)
            dst = jnp.concatenate(d_parts, axis=1)
            acc[at, HD : 2 * HD] += jnp.dot(pt, dos[...], preferred_element_type=jnp.float32)
            acc[at, 0:HD] += jnp.dot(dst, qs[...], preferred_element_type=jnp.float32)
            dqt[...] += lax.dot_general(k, dst, TN, preferred_element_type=jnp.float32)
            return carry2

        lax.fori_loop(0, steps, step, 0)
        for h in range(GROUP):
            part = dqt[:, h * BLK : (h + 1) * BLK] * SCALE
            dq_ref[rows, h * HD : (h + 1) * HD] = part.T.astype(jnp.bfloat16)
        return carry

    lax.fori_loop(0, 2 * SIDE, block, 0)

    def emit(c, carry):
        dkv_ref[span(inverse[c], BLK), :] = acc[pl.ds(pl.multiple_of(PAD + c * BLK, BLK), BLK), :].astype(
            jnp.bfloat16
        )
        return carry

    lax.fori_loop(0, NBLK, emit, 0)


def scatter_kernel(dqx, dkv, dq, dk, dv, own, mid, thr, got, grads, ssem, rsem, lsem):
    a, b, sa, sb = place()
    A = [lax.rem(a + t, SIDE) for t in range(SIDE)]
    B = [lax.rem(b + t, SIDE) for t in range(SIDE)]

    def dev(aa, bb):
        return {"seq": aa * sa + bb * sb}

    def slot(aa, bb):
        return span(aa * sa + bb * sb, ROWS)

    up, down = dev(a, B[1]), dev(a, B[3])
    toward = (up, up, down, down)
    next_b = (B[1], B[1], B[3], B[3])
    loads = [pltpu.make_async_copy(dkv.at[slot(A[t], next_b[t])], mid.at[t], lsem.at[t]) for t in range(SIDE)]
    loads += [pltpu.make_async_copy(dkv.at[slot(A[t], b)], own.at[t], lsem.at[4 + t]) for t in range(SIDE)]
    for load in loads:
        load.start()
    greet([dev(A[1], b), dev(A[3], b), dev(A[2], b), up, down])
    wires = Wires(ssem, rsem)
    through = [wires.send(dkv.at[slot(A[t], B[2])], thr.at[t], toward[t]) for t in range(SIDE)]
    plain = [None] * SIDE
    for t in (2, 3):
        plain[t] = wires.send(dkv.at[slot(A[t], B[1])], got.at[0, t], up)
    for t in (0, 1):
        plain[t] = wires.send(dkv.at[slot(A[t], B[3])], got.at[1, t], down)
    heads = [
        wires.send(dqx.at[span(A[t], ROWS)], dq.at[:, span(a, QW)], dev(A[t], b)) for t in (1, 3, 2)
    ]
    mine = pltpu.make_async_copy(dqx.at[span(a, ROWS)], dq.at[:, span(a, QW)], lsem.at[8])
    mine.start()
    summed = [None] * SIDE
    for t in (0, 2, 1, 3):
        loads[t].wait()
        through[t].wait_recv()
        total = mid[t].astype(jnp.float32) + thr[t].astype(jnp.float32)
        mid[t] = total.astype(jnp.bfloat16)
        side = 0 if t < 2 else 1
        summed[t] = wires.send(mid.at[t], got.at[side, t], toward[t])
    last = []
    copies = []
    for t in (2, 1, 3, 0):
        loads[4 + t].wait()
        plain[t].wait_recv()
        summed[t].wait_recv()
        total = own[t].astype(jnp.float32) + got[0, t].astype(jnp.float32) + got[1, t].astype(jnp.float32)
        grads[t, :, 0:HD] = (total[:, 0:HD] * SCALE).astype(jnp.bfloat16)
        grads[t, :, HD : 2 * HD] = total[:, HD : 2 * HD].astype(jnp.bfloat16)
        for n, d in enumerate((dk, dv)):
            src = grads.at[t, :, pl.ds(n * HD, HD)]
            if t:
                last.append(wires.send(src, d.at[:, span(a, HD)], dev(A[t], b)))
            else:
                copy = pltpu.make_async_copy(src, d.at[:, span(a, HD)], lsem.at[9 + n])
                copy.start()
                copies.append(copy)
    for copy in heads + last:
        copy.wait()
    for copy in through + plain + summed:
        copy.wait_send()
    for copy in copies + [mine]:
        copy.wait()


def gather_call(query, key, value, attn_out, out_grad, log_sums):
    any_spec = pl.BlockSpec(memory_space=pl.ANY)
    bf = jnp.bfloat16
    return pl.pallas_call(
        gather_kernel,
        out_shape=[
            jax.ShapeDtypeStruct((SIDE * ROWS, QW), bf),
            jax.ShapeDtypeStruct((SIDE * ROWS, QW), bf),
            jax.ShapeDtypeStruct((TOKENS, 2 * HD), bf),
            jax.ShapeDtypeStruct((SIDE, 16, ROWS), jnp.float32),
        ],
        in_specs=[any_spec] * 5 + [pl.BlockSpec(memory_space=pltpu.VMEM)],
        out_specs=[any_spec] * 4,
        scratch_shapes=[
            pltpu.VMEM((ROWS, SIDE * QW), bf),
            pltpu.VMEM((ROWS, SIDE * QW), bf),
            pltpu.VMEM((SIDE, 16, ROWS), jnp.float32),
            pltpu.SemaphoreType.DMA((32,)),
            pltpu.SemaphoreType.DMA((32,)),
            pltpu.SemaphoreType.DMA((8,)),
        ],
        compiler_params=pltpu.CompilerParams(
            collective_id=1, has_side_effects=True, vmem_limit_bytes=24 * 2**20
        ),
        name="gather",
    )(query, key, value, attn_out, out_grad, log_sums)


def attend_call(order, docs, qx, dox, aux, kv):
    bf = jnp.bfloat16
    vmem = pl.BlockSpec(memory_space=pltpu.VMEM)
    smem = pl.BlockSpec(memory_space=pltpu.SMEM)
    return pl.pallas_call(
        attend_kernel,
        out_shape=[
            jax.ShapeDtypeStruct((SIDE * ROWS, QW), bf),
            jax.ShapeDtypeStruct((TOKENS, 2 * HD), bf),
        ],
        in_specs=[smem, smem, vmem, vmem, vmem, pl.BlockSpec(memory_space=pl.ANY)],
        out_specs=[vmem, vmem],
        scratch_shapes=[
            pltpu.VMEM((PAD + TOKENS, 2 * HD), bf),
            pltpu.VMEM((PAD + TOKENS, 2 * HD), jnp.float32),
            pltpu.VMEM((QW, HD), bf),
            pltpu.VMEM((QW, HD), bf),
            pltpu.VMEM((HD, QW), jnp.float32),
            pltpu.SMEM((NBLK,), jnp.int32),
            pltpu.SemaphoreType.DMA((NBLK,)),
        ],
        compiler_params=pltpu.CompilerParams(vmem_limit_bytes=48 * 2**20),
        name="attend",
    )(order, docs, qx, dox, aux, kv)


def scatter_call(dqx, dkv):
    bf = jnp.bfloat16
    any_spec = pl.BlockSpec(memory_space=pl.ANY)
    piece = (SIDE, ROWS, 2 * HD)
    return pl.pallas_call(
        scatter_kernel,
        out_shape=[
            jax.ShapeDtypeStruct((ROWS, SIDE * QW), bf),
            jax.ShapeDtypeStruct((ROWS, SIDE * HD), bf),
            jax.ShapeDtypeStruct((ROWS, SIDE * HD), bf),
        ],
        in_specs=[any_spec] * 2,
        out_specs=[any_spec] * 3,
        scratch_shapes=[
            pltpu.VMEM(piece, bf),
            pltpu.VMEM(piece, bf),
            pltpu.VMEM(piece, bf),
            pltpu.VMEM((2,) + piece, bf),
            pltpu.VMEM(piece, bf),
            pltpu.SemaphoreType.DMA((24,)),
            pltpu.SemaphoreType.DMA((24,)),
            pltpu.SemaphoreType.DMA((12,)),
        ],
        compiler_params=pltpu.CompilerParams(
            collective_id=2, has_side_effects=True, vmem_limit_bytes=24 * 2**20
        ),
        name="scatter",
    )(dqx, dkv)


def body(query, key, value, attn_out, out_grad, log_sums, block_order, doc_lengths):
    qx, dox, kv, aux = gather_call(query, key, value, attn_out, out_grad, log_sums)
    dqx, dkv = attend_call(block_order, doc_lengths, qx, dox, aux, kv)
    return scatter_call(dqx, dkv)


def solution(mesh):
    rows = P(("island", "seq"), None)
    return jax.shard_map(
        body,
        mesh=mesh,
        in_specs=(rows,) * 5 + (P(None, ("island", "seq")), P("island"), P("island")),
        out_specs=(rows,) * 3,
        check_vma=False,
    )
```

```python
import functools
import math

import jax
import jax.numpy as jnp
from jax import lax
from jax.experimental import pallas as pl
from jax.experimental.pallas import tpu as pltpu
from jax.sharding import PartitionSpec as P

MESH = pl.DeviceIdType.MESH
HD = 128
BLK = 128
SIDE = 4
ROWS = 256
GROUP = 5
QW = GROUP * HD
TOKENS = 4096
NBLK = 32
PAIR = 2 * BLK
NLOC = 2 * SIDE
SCALE = 1.0 / math.sqrt(HD)
LOG2E = math.log2(math.e)
DEEP = 2
BEFORE = 1
AT = (0, 1, 2, 3)
NT = (((1,), (1,)), ((), ()))
TN = (((0,), (0,)), ((), ()))


def place():
    core = lax.rem(lax.axis_index("island"), 2)
    seq = lax.axis_index("seq")
    x, y = lax.rem(seq, SIDE), seq // SIDE
    a = x + core * (y - x)
    b = y + core * (x - y)
    return a, b, 1 + 3 * core, SIDE - 3 * core


class Wires:
    def __init__(self, send_sems, recv_sems):
        self.send_sems, self.recv_sems, self.count = send_sems, recv_sems, 0

    def send(self, src, dst, device):
        n = self.count
        self.count += 1
        copy = pltpu.make_async_remote_copy(
            src, dst, self.send_sems.at[n], self.recv_sems.at[n], device_id=device, device_id_type=MESH
        )
        copy.start()
        return copy


def span(start, size):
    return pl.ds(pl.multiple_of(start * size, size), size)


def greet(devices):
    barrier = pltpu.get_barrier_semaphore()
    for device in devices:
        pl.semaphore_signal(barrier, inc=1, device_id=device, device_id_type=MESH)
    pl.semaphore_wait(barrier, len(devices))


def weigh(kv, q, do, lse, delta, masks):
    st = lax.dot_general(kv[:, 0:HD], q, NT, preferred_element_type=jnp.float32)
    dpt = lax.dot_general(kv[:, HD : 2 * HD], do, NT, preferred_element_type=jnp.float32)
    probs, dscores = [], []
    for n in range(q.shape[0] // BLK):
        part = slice(n * BLK, (n + 1) * BLK)
        p = jnp.exp2(st[:, part] * (SCALE * LOG2E) - lse[:, part])
        p = jnp.where(masks[n // GROUP], p, 0.0)
        d = p * (dpt[:, part] - delta[:, part])
        probs.append(p.astype(jnp.bfloat16))
        dscores.append(d.astype(jnp.bfloat16))
    return jnp.concatenate(probs, axis=1), jnp.concatenate(dscores, axis=1)


def doc_start(pos, ends):
    begin = jnp.zeros_like(pos)
    for e in ends:
        begin = jnp.where(pos >= e, e, begin)
    return begin


def doc_ends(docs):
    e0 = docs[0]
    e1 = e0 + docs[1]
    return e0, e1, e1 + docs[2]


def gather_kernel(
    order, docs, q_ref, k_ref, v_ref, o_ref, do_ref, lse_ref,
    kv, qs, dos, stats, lkv, ldq,
    o_buf, do_buf, aux, auxx, nq, ndo, nkv, sq, sdo, skv, sstats, sacc, sdq, sj, ssem, rsem, hssem, hrsem, lsem,
):
    a, b, sa, sb = place()
    A = [lax.rem(a + t, SIDE) for t in range(SIDE)]
    B = [lax.rem(b + t, SIDE) for t in range(SIDE)]

    def dev(aa, bb):
        return {"seq": aa * sa + bb * sb}

    def slot(aa, bb):
        return span(aa * sa + bb * sb, ROWS)

    def local(src, dst, n):
        copy = pltpu.make_async_copy(src, dst, lsem.at[n])
        copy.start()
        return copy

    loads = [local(o_ref, o_buf, 0), local(do_ref, do_buf, 1)]
    mine = slot(a, b)
    own_kv = [local(s.at[:, span(a, HD)], kv.at[mine, pl.ds(n * HD, HD)], 2 + n) for n, s in enumerate((k_ref, v_ref))]
    own_q = []
    for h in range(GROUP):
        for n, (s, d) in enumerate(((q_ref, qs), (do_ref, dos))):
            own_q.append(local(s.at[:, span(a * GROUP + h, HD)], d.at[a, h], 4 + 2 * h + n))
    greet([dev(A[1], b), dev(A[3], b), dev(A[2], b), dev(a, B[1]), dev(a, B[3])])
    wires = Wires(ssem, rsem)
    first = {}
    for t in (1, 3, 2):
        first[t] = [
            wires.send(s.at[:, span(A[t], HD)], kv.at[mine, pl.ds(n * HD, HD)], dev(A[t], b))
            for n, s in enumerate((k_ref, v_ref))
        ]
    def head_copy(h, n, t):
        src, dst = ((q_ref, qs), (do_ref, dos))[n]
        sem = (h * 2 + n) * 3 + t - 1
        return pltpu.make_async_remote_copy(
            src.at[:, span(A[t] * GROUP + h, HD)], dst.at[a, h], hssem.at[sem], hrsem.at[sem],
            device_id=dev(A[t], b), device_id_type=MESH,
        )

    def send_head(h):
        for n in range(2):
            for t in (2, 1, 3):
                head_copy(h, n, t).start()

    for h in range(BEFORE):
        send_head(h)

    for load in loads:
        load.wait()
    ones = jnp.ones((8, HD), jnp.bfloat16)
    aux[...] = jnp.zeros_like(aux)
    for g in range(SIDE):
        for h in range(GROUP):
            n = g * GROUP + h
            cols = slice(n * HD, (n + 1) * HD)
            prod = o_buf[:, cols].astype(jnp.float32) * do_buf[:, cols].astype(jnp.float32)
            high = prod.astype(jnp.bfloat16)
            low = (prod - high.astype(jnp.float32)).astype(jnp.bfloat16)
            delta = lax.dot_general(ones, high, NT, preferred_element_type=jnp.float32)
            delta += lax.dot_general(ones, low, NT, preferred_element_type=jnp.float32)
            aux[g, h : h + 1, :] = lse_ref[n : n + 1, :] * LOG2E
            aux[g, 8 + h : 9 + h, :] = delta[0:1]
    facts = [wires.send(aux.at[A[t]], auxx.at[a], dev(A[t], b)) for t in (1, 3, 2)]
    own_q.append(local(aux.at[a], auxx.at[a], 14))
    for h in range(BEFORE, GROUP):
        send_head(h)

    passed = {}

    def spread(t):
        rows = slot(A[t], b)
        passed[t] = (
            wires.send(kv.at[rows], kv.at[rows], dev(a, B[1])),
            wires.send(kv.at[rows], kv.at[rows], dev(a, B[3])),
        )

    for copy in own_kv:
        copy.wait()
    spread(0)
    for t in (1, 3, 2):
        for copy in first[SIDE - t]:
            copy.wait_recv()
        spread(t)
    for copy in own_q + facts:
        copy.wait()
    for m in range(NLOC):
        tok = slice((m % 2) * BLK, (m % 2 + 1) * BLK)
        for h in range(GROUP):
            part = slice(h * BLK, (h + 1) * BLK)
            stats[m, 0:1, part] = auxx[m // 2, h : h + 1, tok]
            stats[m, 1:2, part] = auxx[m // 2, 8 + h : 9 + h, tok]

    ends = doc_ends(docs)
    js = [order[(m // 2 * sa + b * sb) * 2 + m % 2] for m in range(NLOC)]
    ranks = [
        sum((js[i] < js[m] if i > m else js[i] <= js[m]).astype(jnp.int32) for i in range(NLOC) if i != m)
        for m in range(NLOC)
    ]
    for m in range(NLOC):
        nkv[m] = kv[span((m // 2 * sa + b * sb) * 2 + m % 2, BLK), :]
    kinds = [sum(jnp.where(ranks[i] == r, i, 0) for i in range(NLOC)) for r in range(NLOC)]
    for r, m in enumerate(kinds):
        sj[r] = sum(jnp.where(ranks[i] == r, js[i], 0) for i in range(NLOC))
        skv[r * BLK : (r + 1) * BLK, :] = nkv[m]
        facts_r = stats[m]
        for h in range(GROUP):
            sstats[h, :, r * BLK : (r + 1) * BLK] = facts_r[:, h * BLK : (h + 1) * BLK]
    sacc[...] = jnp.zeros_like(sacc)
    iota = lax.broadcasted_iota(jnp.int32, (BLK, BLK), 0)
    kpos = [sj[r] * BLK + iota for r in range(NLOC)]
    qpos = [sj[r] * BLK + lax.broadcasted_iota(jnp.int32, (1, BLK), 1) for r in range(NLOC)]
    qbegin = [doc_start(pos, ends) for pos in qpos]

    second = {}

    def forward(t):
        up, down = passed[t]
        if t in (0, 1):
            up.wait_recv()
            rows = slot(A[t], B[3])
            second[t] = wires.send(kv.at[rows], kv.at[rows], dev(a, B[1]))
        else:
            down.wait_recv()
            rows = slot(A[t], B[1])
            second[t] = wires.send(kv.at[rows], kv.at[rows], dev(a, B[3]))

    def head(h, carry):
        for n in range(2):
            for t in (2, 1, 3):
                head_copy(h, n, t).wait_recv()
        for m in range(NLOC):
            half = slice(m % 2 * BLK, (m % 2 + 1) * BLK)
            nq[m] = qs[m // 2, h, half, :]
            ndo[m] = dos[m // 2, h, half, :]
        for r, m in enumerate(kinds):
            sq[r * BLK : (r + 1) * BLK, :] = nq[m]
            sdo[r * BLK : (r + 1) * BLK, :] = ndo[m]
        st = sstats[h]
        work = []
        for m in range(SIDE):
            keys = skv[0 : (m + 1) * PAIR, :]
            wide = slice(m * PAIR, (m + 1) * PAIR)
            q, do = sq[wide, :], sdo[wide, :]
            sc = lax.dot_general(keys[:, 0:HD], q, NT, preferred_element_type=jnp.float32)
            dp = lax.dot_general(keys[:, HD : 2 * HD], do, NT, preferred_element_type=jnp.float32)
            probs, dscores = [], []
            for u in range(2):
                r = 2 * m + u
                part = slice(u * BLK, (u + 1) * BLK)
                masks = [kpos[n] >= qbegin[r] for n in range(2 * m)]
                masks += [(kpos[n] >= qbegin[r]) & (kpos[n] <= qpos[r]) for n in (2 * m, 2 * m + 1)]
                tok = slice(r * BLK, (r + 1) * BLK)
                p = jnp.exp2(sc[:, part] * (SCALE * LOG2E) - st[0:1, tok])
                p = jnp.where(jnp.concatenate(masks), p, 0.0)
                d = p * (dp[:, part] - st[1:2, tok])
                probs.append(p.astype(jnp.bfloat16))
                dscores.append(d.astype(jnp.bfloat16))
            work.append((keys, q, do, jnp.concatenate(probs, axis=1), jnp.concatenate(dscores, axis=1)))
        for m, (keys, q, do, p, d) in enumerate(work):
            gv = jnp.dot(p, do, preferred_element_type=jnp.float32)
            gk = jnp.dot(d, q, preferred_element_type=jnp.float32)
            for r in range(2 * m + 2):
                rows = slice(r * BLK, (r + 1) * BLK)
                sacc[r, :, HD : 2 * HD] += gv[rows]
                sacc[r, :, 0:HD] += gk[rows]
            g = lax.dot_general(keys[:, 0:HD], d, TN, preferred_element_type=jnp.float32)
            for u in range(2):
                sdq[2 * m + u, h] = g[:, u * BLK : (u + 1) * BLK]
        return carry

    done = 0
    for t, upto in zip((0, 3, 1, 2), AT):
        if upto > done:
            lax.fori_loop(done, upto, head, 0)
            done = upto
        forward(t)
    lax.fori_loop(done, GROUP, head, 0)
    for m in range(NLOC):
        lkv[m] = sacc[ranks[m]]
        ldq[m] = sdq[ranks[m]]

    for t in (0, 1):
        passed[t][1].wait_recv()
    for t in (2, 3):
        passed[t][0].wait_recv()
    for t in range(SIDE):
        second[t].wait()
        for copy in passed[t]:
            copy.wait_send()
    for t in (1, 3, 2):
        for copy in first[t]:
            copy.wait_send()
    for h in range(GROUP):
        for n in range(2):
            for t in (1, 2, 3):
                head_copy(h, n, t).wait_send()


def attend_kernel(order, docs, kv, qs, dos, stats, acc, dqt, inverse, jq, iq, ik):
    a, b, sa, sb = place()
    core = lax.rem(lax.axis_index("island"), 2)
    ends = doc_ends(docs)

    def invert(n, carry):
        inverse[order[n]] = n
        return carry

    lax.fori_loop(0, NBLK, invert, 0, unroll=4)
    acc[...] = jnp.zeros_like(acc)
    dqt[...] = jnp.zeros_like(dqt)

    def plan(i, p):
        j = order[(i // 2 * sa + b * sb) * 2 + lax.rem(i, 2)]
        jq[i] = j
        low = doc_start(j * BLK, ends) // BLK

        def look(c, p):
            seq = inverse[c] // 2
            x, y = lax.rem(seq, SIDE), seq // SIDE
            ik[p] = c
            return p + (y + core * (x - y) != b).astype(jnp.int32)

        q = lax.fori_loop(low, j, look, p)
        ik[q] = -1
        q = q + lax.rem(q, 2)

        def name(t, carry):
            iq[t] = i
            return carry

        lax.fori_loop(p // 2, q // 2, name, 0)
        return q

    total = lax.fori_loop(0, NLOC, plan, 0) // 2
    for u in range(DEEP - 1):
        iq[total + u] = 0
        ik[2 * (total + u)] = -1
        ik[2 * (total + u) + 1] = -1

    def front(t):
        i = iq[t]
        c = [ik[2 * t + u] for u in range(2)]
        at = [span(inverse[jnp.maximum(n, 0)], BLK) for n in c]
        keys = jnp.concatenate([kv[n, :] for n in at])
        q = qs[i // 2, :, span(lax.rem(i, 2), BLK), :].reshape(QW, HD)
        do = dos[i // 2, :, span(lax.rem(i, 2), BLK), :].reshape(QW, HD)
        st = stats[i]
        pos = jq[i] * BLK + lax.broadcasted_iota(jnp.int32, (1, BLK), 1)
        iota = lax.broadcasted_iota(jnp.int32, (BLK, BLK), 0)
        kpos = jnp.concatenate([n * BLK + iota for n in c])
        mask = (kpos >= doc_start(pos, ends)) & (kpos <= pos)
        p, d = weigh(keys, q, do, st[0:1], st[1:2], [mask])
        return i, at, keys, q, do, p, d

    def back(i, at, keys, q, do, p, d):
        gv = jnp.dot(p, do, preferred_element_type=jnp.float32)
        gk = jnp.dot(d, q, preferred_element_type=jnp.float32)
        for n in range(2):
            acc[at[n], HD : 2 * HD] += gv[n * BLK : (n + 1) * BLK]
            acc[at[n], 0:HD] += gk[n * BLK : (n + 1) * BLK]
        dqt[i] += lax.dot_general(keys[:, 0:HD], d, TN, preferred_element_type=jnp.float32)

    def step(s, carry):
        work = [front(s * DEEP + u) for u in range(DEEP)]
        for item in work:
            back(*item)
        return carry

    lax.fori_loop(0, (total + DEEP - 1) // DEEP, step, 0)


def scatter_kernel(
    acc, dqt, lkv, ldq, dq, dk, dv, sent, mid, thr, got, grads, dqs, ssem, rsem, lsem
):
    a, b, sa, sb = place()
    A = [lax.rem(a + t, SIDE) for t in range(SIDE)]
    B = [lax.rem(b + t, SIDE) for t in range(SIDE)]

    def dev(aa, bb):
        return {"seq": aa * sa + bb * sb}

    def slot(aa, bb):
        return span(aa * sa + bb * sb, ROWS)

    up, down = dev(a, B[1]), dev(a, B[3])
    toward = (up, up, down, down)
    next_b = (B[1], B[1], B[3], B[3])
    other_b = (B[3], B[3], B[1], B[1])
    other = (down, down, up, up)
    for t in range(SIDE):
        sent[t] = acc[slot(A[t], B[2]), :].astype(jnp.bfloat16)
    greet([dev(A[1], b), dev(A[3], b), dev(A[2], b), up, down])
    wires = Wires(ssem, rsem)
    through = [wires.send(sent.at[t], thr.at[t], toward[t]) for t in range(SIDE)]
    plain = [None] * SIDE
    for t in (0, 2, 1, 3):
        sent[SIDE + t] = acc[slot(A[t], other_b[t]), :].astype(jnp.bfloat16)
        plain[t] = wires.send(sent.at[SIDE + t], got.at[1 if t < 2 else 0, t], other[t])

    def finish(t):
        for u in range(2):
            m = 2 * A[t] + u
            for h in range(GROUP):
                part = slice(h * BLK, (h + 1) * BLK)
                g = (dqt[m, :, part] + ldq[m, h]) * SCALE
                dqs[t, u * BLK : (u + 1) * BLK, part] = g.T.astype(jnp.bfloat16)

    heads = []
    for t in (2, 1, 3):
        finish(t)
        heads.append(wires.send(dqs.at[t], dq.at[:, span(a, QW)], dev(A[t], b)))
    summed = [None] * SIDE
    for t in (0, 2, 1, 3):
        through[t].wait_recv()
        total = acc[slot(A[t], next_b[t]), :] + thr[t].astype(jnp.float32)
        mid[t] = total.astype(jnp.bfloat16)
        summed[t] = wires.send(mid.at[t], got.at[0 if t < 2 else 1, t], toward[t])
    finish(0)
    copies = [pltpu.make_async_copy(dqs.at[0], dq.at[:, span(a, QW)], lsem.at[0])]
    copies[0].start()
    last = []
    for t in (2, 1, 3, 0):
        plain[t].wait_recv()
        summed[t].wait_recv()
        own = lkv[pl.ds(2 * A[t], 2)].reshape(ROWS, 2 * HD)
        total = own + got[0, t].astype(jnp.float32) + got[1, t].astype(jnp.float32)
        grads[t, :, 0:HD] = (total[:, 0:HD] * SCALE).astype(jnp.bfloat16)
        grads[t, :, HD : 2 * HD] = total[:, HD : 2 * HD].astype(jnp.bfloat16)
        for n, d in enumerate((dk, dv)):
            src = grads.at[t, :, pl.ds(n * HD, HD)]
            if t:
                last.append(wires.send(src, d.at[:, span(a, HD)], dev(A[t], b)))
            else:
                copy = pltpu.make_async_copy(src, d.at[:, span(a, HD)], lsem.at[1 + n])
                copy.start()
                copies.append(copy)
    for copy in heads + last:
        copy.wait()
    for copy in through + plain + summed:
        copy.wait_send()
    for copy in copies:
        copy.wait()


ANY = pl.BlockSpec(memory_space=pl.ANY)
HBM = pl.BlockSpec(memory_space=pltpu.HBM)
VMEM = pl.BlockSpec(memory_space=pltpu.VMEM)
SMEM = pl.BlockSpec(memory_space=pltpu.SMEM)
BF = jnp.bfloat16
F32 = jnp.float32
MIB = 2**20


def shapes(*pairs):
    return [jax.ShapeDtypeStruct(s, d) for s, d in pairs]


def gather_call(order, docs, query, key, value, attn_out, out_grad, log_sums):
    packed = (SIDE, GROUP, ROWS, HD)
    return pl.pallas_call(
        gather_kernel,
        out_shape=shapes(
            ((TOKENS, 2 * HD), BF), (packed, BF), (packed, BF), ((NLOC, 8, QW), F32),
            ((NLOC, BLK, 2 * HD), F32), ((NLOC, GROUP, HD, BLK), F32),
        ),
        in_specs=[SMEM, SMEM] + [HBM] * 5 + [VMEM],
        out_specs=[VMEM] * 6,
        scratch_shapes=[
            pltpu.VMEM((ROWS, SIDE * QW), BF),
            pltpu.VMEM((ROWS, SIDE * QW), BF),
            pltpu.VMEM((SIDE, 16, ROWS), F32),
            pltpu.VMEM((SIDE, 16, ROWS), F32),
            pltpu.VMEM((NLOC, BLK, HD), BF),
            pltpu.VMEM((NLOC, BLK, HD), BF),
            pltpu.VMEM((NLOC, BLK, 2 * HD), BF),
            pltpu.VMEM((NLOC * BLK, HD), BF),
            pltpu.VMEM((NLOC * BLK, HD), BF),
            pltpu.VMEM((NLOC * BLK, 2 * HD), BF),
            pltpu.VMEM((GROUP, 8, NLOC * BLK), F32),
            pltpu.VMEM((NLOC, BLK, 2 * HD), F32),
            pltpu.VMEM((NLOC, GROUP, HD, BLK), F32),
            pltpu.SMEM((NLOC,), jnp.int32),
            pltpu.SemaphoreType.DMA((24,)),
            pltpu.SemaphoreType.DMA((24,)),
            pltpu.SemaphoreType.DMA((30,)),
            pltpu.SemaphoreType.DMA((30,)),
            pltpu.SemaphoreType.DMA((16,)),
        ],
        compiler_params=pltpu.CompilerParams(
            collective_id=1, has_side_effects=True, vmem_limit_bytes=49 * MIB
        ),
        name="gather",
    )(order, docs, query, key, value, attn_out, out_grad, log_sums)


def attend_call(order, docs, kv, qs, dos, stats):
    return pl.pallas_call(
        attend_kernel,
        out_shape=shapes(((TOKENS, 2 * HD), F32), ((NLOC, HD, QW), F32)),
        in_specs=[SMEM, SMEM] + [VMEM] * 4,
        out_specs=[VMEM, VMEM],
        scratch_shapes=[
            pltpu.SMEM((NBLK,), jnp.int32),
            pltpu.SMEM((NLOC,), jnp.int32),
            pltpu.SMEM((128,), jnp.int32),
            pltpu.SMEM((256,), jnp.int32),
        ],
        compiler_params=pltpu.CompilerParams(vmem_limit_bytes=28 * MIB),
        name="attend",
    )(order, docs, kv, qs, dos, stats)


def scatter_call(acc, dqt, lkv, ldq):
    piece = (SIDE, ROWS, 2 * HD)
    return pl.pallas_call(
        scatter_kernel,
        out_shape=shapes(((ROWS, SIDE * QW), BF), ((ROWS, SIDE * HD), BF), ((ROWS, SIDE * HD), BF)),
        in_specs=[VMEM] * 4,
        out_specs=[ANY] * 3,
        scratch_shapes=[
            pltpu.VMEM((2 * SIDE, ROWS, 2 * HD), BF),
            pltpu.VMEM(piece, BF),
            pltpu.VMEM(piece, BF),
            pltpu.VMEM((2,) + piece, BF),
            pltpu.VMEM(piece, BF),
            pltpu.VMEM((SIDE, ROWS, QW), BF),
            pltpu.SemaphoreType.DMA((24,)),
            pltpu.SemaphoreType.DMA((24,)),
            pltpu.SemaphoreType.DMA((4,)),
        ],
        compiler_params=pltpu.CompilerParams(
            collective_id=2, has_side_effects=True, vmem_limit_bytes=28 * MIB
        ),
        name="scatter",
    )(acc, dqt, lkv, ldq)


def body(query, key, value, attn_out, out_grad, log_sums, block_order, doc_lengths):
    kv, qs, dos, stats, lkv, ldq = gather_call(
        block_order, doc_lengths, query, key, value, attn_out, out_grad, log_sums
    )
    acc, dqt = attend_call(block_order, doc_lengths, kv, qs, dos, stats)
    return scatter_call(acc, dqt, lkv, ldq)


def solution(mesh):
    rows = P(("island", "seq"), None)
    return jax.shard_map(
        body,
        mesh=mesh,
        in_specs=(rows,) * 5 + (P(None, ("island", "seq")), P("island"), P("island")),
        out_specs=(rows,) * 3,
        check_vma=False,
    )
```

```python
import functools
import math

import jax
import jax.numpy as jnp
from jax import lax
from jax.experimental import pallas as pl
from jax.experimental.pallas import tpu as pltpu
from jax.sharding import PartitionSpec as P

MESH = pl.DeviceIdType.MESH
HD = 128
BLK = 128
SIDE = 4
ROWS = 256
GROUP = 5
QW = GROUP * HD
TOKENS = 4096
NBLK = 32
PAIR = 2 * BLK
NLOC = 2 * SIDE
SCALE = 1.0 / math.sqrt(HD)
LOG2E = math.log2(math.e)
DEEP = 4
BEFORE = 1
AT = (1, 2, 3, 4)
NT = (((1,), (1,)), ((), ()))
TN = (((0,), (0,)), ((), ()))


def place():
    core = lax.rem(lax.axis_index("island"), 2)
    seq = lax.axis_index("seq")
    x, y = lax.rem(seq, SIDE), seq // SIDE
    a = x + core * (y - x)
    b = y + core * (x - y)
    return a, b, 1 + 3 * core, SIDE - 3 * core


class Wires:
    def __init__(self, send_sems, recv_sems):
        self.send_sems, self.recv_sems, self.count = send_sems, recv_sems, 0

    def send(self, src, dst, device):
        n = self.count
        self.count += 1
        copy = pltpu.make_async_remote_copy(
            src, dst, self.send_sems.at[n], self.recv_sems.at[n], device_id=device, device_id_type=MESH
        )
        copy.start()
        return copy


def span(start, size):
    return pl.ds(pl.multiple_of(start * size, size), size)


def greet(devices):
    barrier = pltpu.get_barrier_semaphore()
    for device in devices:
        pl.semaphore_signal(barrier, inc=1, device_id=device, device_id_type=MESH)
    pl.semaphore_wait(barrier, len(devices))


def weigh(keys, values, q, do, lse, delta, mask):
    st = lax.dot_general(keys, q, NT, preferred_element_type=jnp.float32)
    dpt = lax.dot_general(values, do, NT, preferred_element_type=jnp.float32)
    probs, dscores = [], []
    for n in range(q.shape[0] // BLK):
        part = slice(n * BLK, (n + 1) * BLK)
        p = jnp.exp2(st[:, part] * (SCALE * LOG2E) - lse[:, part])
        p = jnp.where(mask, p, 0.0)
        d = p * (dpt[:, part] - delta[:, part])
        probs.append(p.astype(jnp.bfloat16))
        dscores.append(d.astype(jnp.bfloat16))
    return jnp.concatenate(probs, axis=1), jnp.concatenate(dscores, axis=1)


def doc_start(pos, ends):
    begin = jnp.zeros_like(pos)
    for e in ends:
        begin = jnp.where(pos >= e, e, begin)
    return begin


def doc_ends(facts):
    e0 = facts[NBLK]
    e1 = e0 + facts[NBLK + 1]
    return e0, e1, e1 + facts[NBLK + 2]


def gather_kernel(
    facts_ref, q_ref, kv_ref, o_ref, do_ref, lse_ref,
    ks, vs, qs, dos, stats, lkv, l0, l1, l2, l3, l4,
    o_buf, do_buf, aux, auxx, nq, ndo, nkv, sq, sdo, skv, sstats, sacc, sdq, sj, ssem, rsem, hssem, hrsem, lsem,
):
    a, b, sa, sb = place()
    A = [lax.rem(a + t, SIDE) for t in range(SIDE)]
    B = [lax.rem(b + t, SIDE) for t in range(SIDE)]

    def dev(aa, bb):
        return {"seq": aa * sa + bb * sb}

    def slot(aa, bb):
        return span(aa * sa + bb * sb, ROWS)

    kvs = (ks, vs)
    ldq = (l0, l1, l2, l3, l4)

    def local(src, dst, n):
        copy = pltpu.make_async_copy(src, dst, lsem.at[n])
        copy.start()
        return copy

    loads = [local(o_ref, o_buf, 0), local(do_ref, do_buf, 1)]
    mine = slot(a, b)
    own_kv = [local(kv_ref.at[:, span(a + SIDE * n, HD)], kvs[n].at[mine], 2 + n) for n in range(2)]
    own_q = []
    for h in range(GROUP):
        for n, (s, d) in enumerate(((q_ref, qs), (do_ref, dos))):
            own_q.append(local(s.at[:, span(a * GROUP + h, HD)], d.at[a, h], 4 + 2 * h + n))
    greet([dev(A[1], b), dev(A[3], b), dev(A[2], b), dev(a, B[1]), dev(a, B[3])])
    wires = Wires(ssem, rsem)
    first = {}
    for t in (1, 3, 2):
        first[t] = [
            wires.send(kv_ref.at[:, span(A[t] + SIDE * n, HD)], kvs[n].at[mine], dev(A[t], b))
            for n in range(2)
        ]
    def head_copy(h, n, t):
        src, dst = ((q_ref, qs), (do_ref, dos))[n]
        sem = (h * 2 + n) * 3 + t - 1
        return pltpu.make_async_remote_copy(
            src.at[:, span(A[t] * GROUP + h, HD)], dst.at[a, h], hssem.at[sem], hrsem.at[sem],
            device_id=dev(A[t], b), device_id_type=MESH,
        )

    def send_head(h):
        for n in range(2):
            for t in (2, 1, 3):
                head_copy(h, n, t).start()

    for h in range(BEFORE):
        send_head(h)

    for load in loads:
        load.wait()
    ones = jnp.ones((8, HD), jnp.bfloat16)
    aux[...] = jnp.zeros_like(aux)
    for g in range(SIDE):
        for h in range(GROUP):
            n = g * GROUP + h
            cols = slice(n * HD, (n + 1) * HD)
            prod = o_buf[:, cols].astype(jnp.float32) * do_buf[:, cols].astype(jnp.float32)
            high = prod.astype(jnp.bfloat16)
            low = (prod - high.astype(jnp.float32)).astype(jnp.bfloat16)
            delta = lax.dot_general(ones, high, NT, preferred_element_type=jnp.float32)
            delta += lax.dot_general(ones, low, NT, preferred_element_type=jnp.float32)
            aux[g, h : h + 1, :] = lse_ref[n : n + 1, :] * LOG2E
            aux[g, 8 + h : 9 + h, :] = delta[0:1]
    facts = [wires.send(aux.at[A[t]], auxx.at[a], dev(A[t], b)) for t in (1, 3, 2)]
    own_q.append(local(aux.at[a], auxx.at[a], 14))
    for h in range(BEFORE, GROUP):
        send_head(h)

    passed = {}

    def spread(t):
        rows = slot(A[t], b)
        passed[t] = [[wires.send(x.at[rows], x.at[rows], dev(a, B[n])) for x in kvs] for n in (1, 3)]

    for copy in own_kv:
        copy.wait()
    spread(0)
    for t in (1, 3, 2):
        for copy in first[SIDE - t]:
            copy.wait_recv()
        spread(t)
    for copy in own_q + facts:
        copy.wait()
    for m in range(NLOC):
        tok = slice((m % 2) * BLK, (m % 2 + 1) * BLK)
        for h in range(GROUP):
            part = slice(h * BLK, (h + 1) * BLK)
            stats[m, 0:1, part] = auxx[m // 2, h : h + 1, tok]
            stats[m, 1:2, part] = auxx[m // 2, 8 + h : 9 + h, tok]

    order = facts_ref
    ends = doc_ends(order)
    js = [order[(m // 2 * sa + b * sb) * 2 + m % 2] for m in range(NLOC)]
    ranks = [
        sum((js[i] < js[m] if i > m else js[i] <= js[m]).astype(jnp.int32) for i in range(NLOC) if i != m)
        for m in range(NLOC)
    ]
    for m in range(NLOC):
        here = span((m // 2 * sa + b * sb) * 2 + m % 2, BLK)
        nkv[m] = jnp.concatenate([ks[here, :], vs[here, :]], axis=1)
    kinds = [sum(jnp.where(ranks[i] == r, i, 0) for i in range(NLOC)) for r in range(NLOC)]
    for r, m in enumerate(kinds):
        sj[r] = sum(jnp.where(ranks[i] == r, js[i], 0) for i in range(NLOC))
        skv[r * BLK : (r + 1) * BLK, :] = nkv[m]
        facts_r = stats[m]
        for h in range(GROUP):
            sstats[h, :, r * BLK : (r + 1) * BLK] = facts_r[:, h * BLK : (h + 1) * BLK]
    sacc[...] = jnp.zeros_like(sacc)
    iota = lax.broadcasted_iota(jnp.int32, (BLK, BLK), 0)
    kpos = [sj[r] * BLK + iota for r in range(NLOC)]
    qpos = [sj[r] * BLK + lax.broadcasted_iota(jnp.int32, (1, BLK), 1) for r in range(NLOC)]
    qbegin = [doc_start(pos, ends) for pos in qpos]

    second = {}

    def forward(t):
        up, down = passed[t]
        for copy in up if t < 2 else down:
            copy.wait_recv()
        rows = slot(A[t], B[3] if t < 2 else B[1])
        second[t] = [wires.send(x.at[rows], x.at[rows], dev(a, B[1] if t < 2 else B[3])) for x in kvs]

    def head(h, carry):
        for n in range(2):
            for t in (2, 1, 3):
                head_copy(h, n, t).wait_recv()
        for m in range(NLOC):
            half = slice(m % 2 * BLK, (m % 2 + 1) * BLK)
            nq[m] = qs[m // 2, h, half, :]
            ndo[m] = dos[m // 2, h, half, :]
        for r, m in enumerate(kinds):
            sq[r * BLK : (r + 1) * BLK, :] = nq[m]
            sdo[r * BLK : (r + 1) * BLK, :] = ndo[m]
        st = sstats[h]
        work = []
        for m in range(SIDE):
            keys = skv[0 : (m + 1) * PAIR, :]
            wide = slice(m * PAIR, (m + 1) * PAIR)
            q, do = sq[wide, :], sdo[wide, :]
            sc = lax.dot_general(keys[:, 0:HD], q, NT, preferred_element_type=jnp.float32)
            dp = lax.dot_general(keys[:, HD : 2 * HD], do, NT, preferred_element_type=jnp.float32)
            probs, dscores = [], []
            for u in range(2):
                r = 2 * m + u
                part = slice(u * BLK, (u + 1) * BLK)
                masks = [kpos[n] >= qbegin[r] for n in range(2 * m)]
                masks += [(kpos[n] >= qbegin[r]) & (kpos[n] <= qpos[r]) for n in (2 * m, 2 * m + 1)]
                tok = slice(r * BLK, (r + 1) * BLK)
                p = jnp.exp2(sc[:, part] * (SCALE * LOG2E) - st[0:1, tok])
                p = jnp.where(jnp.concatenate(masks), p, 0.0)
                d = p * (dp[:, part] - st[1:2, tok])
                probs.append(p.astype(jnp.bfloat16))
                dscores.append(d.astype(jnp.bfloat16))
            work.append((keys, q, do, jnp.concatenate(probs, axis=1), jnp.concatenate(dscores, axis=1)))
        for m, (keys, q, do, p, d) in enumerate(work):
            gv = jnp.dot(p, do, preferred_element_type=jnp.float32)
            gk = jnp.dot(d, q, preferred_element_type=jnp.float32)
            for r in range(2 * m + 2):
                rows = slice(r * BLK, (r + 1) * BLK)
                sacc[r, :, HD : 2 * HD] += gv[rows]
                sacc[r, :, 0:HD] += gk[rows]
            g = lax.dot_general(keys[:, 0:HD], d, TN, preferred_element_type=jnp.float32)
            for u in range(2):
                sdq[2 * m + u, h] = g[:, u * BLK : (u + 1) * BLK]
        return carry

    done = 0
    for t, upto in zip((0, 3, 1, 2), AT):
        if upto > done:
            lax.fori_loop(done, upto, head, 0)
            done = upto
        forward(t)
    lax.fori_loop(done, GROUP, head, 0)
    for m in range(NLOC):
        lkv[m] = sacc[ranks[m]]
        mine_dq = sdq[ranks[m]]
        for h in range(GROUP):
            ldq[h][m] = mine_dq[h]

    for t in range(SIDE):
        for copy in passed[t][1 if t < 2 else 0]:
            copy.wait_recv()
        for copy in second[t]:
            copy.wait()
        for copy in passed[t][0] + passed[t][1]:
            copy.wait_send()
    for t in (1, 3, 2):
        for copy in first[t]:
            copy.wait_send()
    for h in range(GROUP):
        for n in range(2):
            for t in (1, 2, 3):
                head_copy(h, n, t).wait_send()


def attend_kernel(order, ks, vs, qs, dos, stats, acc, dqt, inverse, jq, iq, ik):
    a, b, sa, sb = place()
    core = lax.rem(lax.axis_index("island"), 2)
    ends = doc_ends(order)

    def invert(n, carry):
        inverse[order[n]] = n
        return carry

    lax.fori_loop(0, NBLK, invert, 0, unroll=4)
    acc[...] = jnp.zeros_like(acc)
    dqt[...] = jnp.zeros_like(dqt)

    def plan(i, p):
        j = order[(i // 2 * sa + b * sb) * 2 + lax.rem(i, 2)]
        jq[i] = j
        low = doc_start(j * BLK, ends) // BLK

        def look(c, p):
            seq = inverse[c] // 2
            x, y = lax.rem(seq, SIDE), seq // SIDE
            ik[p] = c
            return p + (y + core * (x - y) != b).astype(jnp.int32)

        q = lax.fori_loop(low, j, look, p)
        ik[q] = -1
        q = q + lax.rem(q, 2)

        def name(t, carry):
            iq[t] = i
            return carry

        lax.fori_loop(p // 2, q // 2, name, 0)
        return q

    total = lax.fori_loop(0, NLOC, plan, 0) // 2
    def front(t):
        i = iq[t]
        c = [ik[2 * t + u] for u in range(2)]
        at = [span(inverse[jnp.maximum(n, 0)], BLK) for n in c]
        keys = jnp.concatenate([ks[n, :] for n in at])
        values = jnp.concatenate([vs[n, :] for n in at])
        q = qs[i // 2, :, span(lax.rem(i, 2), BLK), :].reshape(QW, HD)
        do = dos[i // 2, :, span(lax.rem(i, 2), BLK), :].reshape(QW, HD)
        st = stats[i]
        pos = jq[i] * BLK + lax.broadcasted_iota(jnp.int32, (1, BLK), 1)
        iota = lax.broadcasted_iota(jnp.int32, (BLK, BLK), 0)
        kpos = jnp.concatenate([n * BLK + iota for n in c])
        mask = (kpos >= doc_start(pos, ends)) & (kpos <= pos)
        p, d = weigh(keys, values, q, do, st[0:1], st[1:2], mask)
        return i, at, keys, q, do, p, d

    def back(i, at, keys, q, do, p, d):
        gv = jnp.dot(p, do, preferred_element_type=jnp.float32)
        gk = jnp.dot(d, q, preferred_element_type=jnp.float32)
        for n in range(2):
            acc[at[n], HD : 2 * HD] += gv[n * BLK : (n + 1) * BLK]
            acc[at[n], 0:HD] += gk[n * BLK : (n + 1) * BLK]
        dqt[i] += lax.dot_general(keys, d, TN, preferred_element_type=jnp.float32)

    def group(first, size):
        held = front(first)
        for u in range(1, size):
            following = front(first + u)
            back(*held)
            held = following
        back(*held)

    def step(s, carry):
        group(s * DEEP, DEEP)
        return carry

    def single(s, carry):
        group(s, 1)
        return carry

    lax.fori_loop(0, total // DEEP, step, 0)
    lax.fori_loop(total // DEEP * DEEP, total, single, 0)


def scatter_kernel(
    acc, dqt, lkv, l0, l1, l2, l3, l4, dq, dk, dv, sent, mid, thr, got, grads, dqs, ssem, rsem, lsem
):
    a, b, sa, sb = place()
    A = [lax.rem(a + t, SIDE) for t in range(SIDE)]
    B = [lax.rem(b + t, SIDE) for t in range(SIDE)]

    def dev(aa, bb):
        return {"seq": aa * sa + bb * sb}

    def slot(aa, bb):
        return span(aa * sa + bb * sb, ROWS)

    up, down = dev(a, B[1]), dev(a, B[3])
    toward = (up, up, down, down)
    next_b = (B[1], B[1], B[3], B[3])
    other_b = (B[3], B[3], B[1], B[1])
    other = (down, down, up, up)
    for t in range(SIDE):
        sent[t] = acc[slot(A[t], B[2]), :].astype(jnp.bfloat16)
    greet([dev(A[1], b), dev(A[3], b), dev(A[2], b), up, down])
    wires = Wires(ssem, rsem)
    through = [wires.send(sent.at[t], thr.at[t], toward[t]) for t in range(SIDE)]
    plain = [None] * SIDE
    for t in (0, 2, 1, 3):
        sent[SIDE + t] = acc[slot(A[t], other_b[t]), :].astype(jnp.bfloat16)
        plain[t] = wires.send(sent.at[SIDE + t], got.at[1 if t < 2 else 0, t], other[t])

    def finish(t):
        for u in range(2):
            m = 2 * A[t] + u
            for h in range(GROUP):
                part = slice(h * BLK, (h + 1) * BLK)
                g = (dqt[m, :, part] + (l0, l1, l2, l3, l4)[h][m]) * SCALE
                dqs[t, u * BLK : (u + 1) * BLK, part] = g.T.astype(jnp.bfloat16)

    heads = []
    for t in (2, 1, 3):
        finish(t)
        heads.append(wires.send(dqs.at[t], dq.at[:, span(a, QW)], dev(A[t], b)))
    summed = [None] * SIDE
    for t in (0, 2, 1, 3):
        through[t].wait_recv()
        total = acc[slot(A[t], next_b[t]), :] + thr[t].astype(jnp.float32)
        mid[t] = total.astype(jnp.bfloat16)
        summed[t] = wires.send(mid.at[t], got.at[0 if t < 2 else 1, t], toward[t])
    finish(0)
    copies = [pltpu.make_async_copy(dqs.at[0], dq.at[:, span(a, QW)], lsem.at[0])]
    copies[0].start()
    last = []
    for t in (2, 1, 3, 0):
        plain[t].wait_recv()
        summed[t].wait_recv()
        own = lkv[pl.ds(2 * A[t], 2)].reshape(ROWS, 2 * HD)
        total = own + got[0, t].astype(jnp.float32) + got[1, t].astype(jnp.float32)
        grads[t, :, 0:HD] = (total[:, 0:HD] * SCALE).astype(jnp.bfloat16)
        grads[t, :, HD : 2 * HD] = total[:, HD : 2 * HD].astype(jnp.bfloat16)
        for n, d in enumerate((dk, dv)):
            src = grads.at[t, :, pl.ds(n * HD, HD)]
            if t:
                last.append(wires.send(src, d.at[:, span(a, HD)], dev(A[t], b)))
            else:
                copy = pltpu.make_async_copy(src, d.at[:, span(a, HD)], lsem.at[1 + n])
                copy.start()
                copies.append(copy)
    for copy in heads + last:
        copy.wait()
    for copy in through + plain + summed:
        copy.wait_send()
    for copy in copies:
        copy.wait()


def emit_kernel(*refs):
    sems = refs[-1]
    copies = [pltpu.make_async_copy(refs[n], refs[n + 3], sems.at[n]) for n in range(3)]
    for copy in copies:
        copy.start()
    for copy in copies:
        copy.wait()


ANY = pl.BlockSpec(memory_space=pl.ANY)
HBM = pl.BlockSpec(memory_space=pltpu.HBM)
VMEM = pl.BlockSpec(memory_space=pltpu.VMEM)
SMEM = pl.BlockSpec(memory_space=pltpu.SMEM)
BF = jnp.bfloat16
F32 = jnp.float32
MIB = 2**20


def shapes(*pairs):
    return [jax.ShapeDtypeStruct(s, d) for s, d in pairs]


def gather_call(facts, query, kv, attn_out, out_grad, log_sums):
    packed = (SIDE, GROUP, ROWS, HD)
    return pl.pallas_call(
        gather_kernel,
        out_shape=shapes(
            ((TOKENS, HD), BF), ((TOKENS, HD), BF), (packed, BF), (packed, BF), ((NLOC, 8, QW), F32),
            ((NLOC, BLK, 2 * HD), F32), *[((NLOC, HD, BLK), F32)] * GROUP,
        ),
        in_specs=[SMEM] + [HBM] * 4 + [VMEM],
        out_specs=[VMEM] * 11,
        scratch_shapes=[
            pltpu.VMEM((ROWS, SIDE * QW), BF),
            pltpu.VMEM((ROWS, SIDE * QW), BF),
            pltpu.VMEM((SIDE, 16, ROWS), F32),
            pltpu.VMEM((SIDE, 16, ROWS), F32),
            pltpu.VMEM((NLOC, BLK, HD), BF),
            pltpu.VMEM((NLOC, BLK, HD), BF),
            pltpu.VMEM((NLOC, BLK, 2 * HD), BF),
            pltpu.VMEM((NLOC * BLK, HD), BF),
            pltpu.VMEM((NLOC * BLK, HD), BF),
            pltpu.VMEM((NLOC * BLK, 2 * HD), BF),
            pltpu.VMEM((GROUP, 8, NLOC * BLK), F32),
            pltpu.VMEM((NLOC, BLK, 2 * HD), F32),
            pltpu.VMEM((NLOC, GROUP, HD, BLK), F32),
            pltpu.SMEM((NLOC,), jnp.int32),
            pltpu.SemaphoreType.DMA((40,)),
            pltpu.SemaphoreType.DMA((40,)),
            pltpu.SemaphoreType.DMA((30,)),
            pltpu.SemaphoreType.DMA((30,)),
            pltpu.SemaphoreType.DMA((16,)),
        ],
        compiler_params=pltpu.CompilerParams(
            collective_id=1, has_side_effects=True, vmem_limit_bytes=45 * MIB
        ),
        name="gather",
    )(facts, query, kv, attn_out, out_grad, log_sums)


def attend_call(facts, ks, vs, qs, dos, stats):
    return pl.pallas_call(
        attend_kernel,
        out_shape=shapes(((TOKENS, 2 * HD), F32), ((NLOC, HD, QW), F32)),
        in_specs=[SMEM] + [VMEM] * 5,
        out_specs=[VMEM, VMEM],
        scratch_shapes=[
            pltpu.SMEM((NBLK,), jnp.int32),
            pltpu.SMEM((NLOC,), jnp.int32),
            pltpu.SMEM((128,), jnp.int32),
            pltpu.SMEM((256,), jnp.int32),
        ],
        compiler_params=pltpu.CompilerParams(vmem_limit_bytes=28 * MIB),
        name="attend",
    )(facts, ks, vs, qs, dos, stats)


def scatter_call(acc, dqt, lkv, *ldq):
    piece = (SIDE, ROWS, 2 * HD)
    return pl.pallas_call(
        scatter_kernel,
        out_shape=shapes(((ROWS, SIDE * QW), BF), ((ROWS, SIDE * HD), BF), ((ROWS, SIDE * HD), BF)),
        in_specs=[VMEM] * 8,
        out_specs=[ANY] * 3,
        scratch_shapes=[
            pltpu.VMEM((2 * SIDE, ROWS, 2 * HD), BF),
            pltpu.VMEM(piece, BF),
            pltpu.VMEM(piece, BF),
            pltpu.VMEM((2,) + piece, BF),
            pltpu.VMEM(piece, BF),
            pltpu.VMEM((SIDE, ROWS, QW), BF),
            pltpu.SemaphoreType.DMA((24,)),
            pltpu.SemaphoreType.DMA((24,)),
            pltpu.SemaphoreType.DMA((4,)),
        ],
        compiler_params=pltpu.CompilerParams(
            collective_id=2, has_side_effects=True, vmem_limit_bytes=28 * MIB
        ),
        name="scatter",
    )(acc, dqt, lkv, *ldq)


def emit_call(*grads):
    return pl.pallas_call(
        emit_kernel,
        out_shape=shapes(*((g.shape, g.dtype) for g in grads)),
        in_specs=[VMEM] * 3,
        out_specs=[HBM] * 3,
        scratch_shapes=[pltpu.SemaphoreType.DMA((3,))],
        compiler_params=pltpu.CompilerParams(vmem_limit_bytes=4 * MIB),
        name="emit",
    )(*grads)


def body(query, key, value, attn_out, out_grad, log_sums, block_order, doc_lengths):
    facts = jnp.concatenate([block_order, doc_lengths])
    kv = jnp.concatenate([key, value], axis=1)
    ks, vs, qs, dos, stats, lkv, *ldq = gather_call(facts, query, kv, attn_out, out_grad, log_sums)
    acc, dqt = attend_call(facts, ks, vs, qs, dos, stats)
    return emit_call(*scatter_call(acc, dqt, lkv, *ldq))


def solution(mesh):
    rows = P(("island", "seq"), None)
    return jax.shard_map(
        body,
        mesh=mesh,
        in_specs=(rows,) * 5 + (P(None, ("island", "seq")), P("island"), P("island")),
        out_specs=(rows,) * 3,
        check_vma=False,
    )
```

```python
import functools
import math

import jax
import jax.numpy as jnp
from jax import lax
from jax.experimental import pallas as pl
from jax.experimental.pallas import tpu as pltpu
from jax.sharding import PartitionSpec as P

MESH = pl.DeviceIdType.MESH
HD = 128
BLK = 128
SIDE = 4
ROWS = 256
GROUP = 5
QW = GROUP * HD
TOKENS = 4096
NBLK = 32
PAIR = 2 * BLK
NLOC = 2 * SIDE
SCALE = 1.0 / math.sqrt(HD)
LOG2E = math.log2(math.e)
DEEP = 4
BEFORE = 1
AT = (1, 2, 3, 4)
NT = (((1,), (1,)), ((), ()))
TN = (((0,), (0,)), ((), ()))


def place():
    core = lax.rem(lax.axis_index("island"), 2)
    seq = lax.axis_index("seq")
    x, y = lax.rem(seq, SIDE), seq // SIDE
    a = x + core * (y - x)
    b = y + core * (x - y)
    return a, b, 1 + 3 * core, SIDE - 3 * core


class Wires:
    def __init__(self, send_sems, recv_sems):
        self.send_sems, self.recv_sems, self.count = send_sems, recv_sems, 0

    def send(self, src, dst, device):
        n = self.count
        self.count += 1
        copy = pltpu.make_async_remote_copy(
            src, dst, self.send_sems.at[n], self.recv_sems.at[n], device_id=device, device_id_type=MESH
        )
        copy.start()
        return copy


def span(start, size):
    return pl.ds(pl.multiple_of(start * size, size), size)


def greet(devices):
    barrier = pltpu.get_barrier_semaphore()
    for device in devices:
        pl.semaphore_signal(barrier, inc=1, device_id=device, device_id_type=MESH)
    pl.semaphore_wait(barrier, len(devices))


def weigh(keys, values, q, do, lse, delta, mask):
    st = lax.dot_general(keys, q, NT, preferred_element_type=jnp.float32)
    dpt = lax.dot_general(values, do, NT, preferred_element_type=jnp.float32)
    probs, dscores = [], []
    for n in range(q.shape[0] // BLK):
        part = slice(n * BLK, (n + 1) * BLK)
        p = jnp.exp2(st[:, part] * (SCALE * LOG2E) - lse[:, part])
        p = jnp.where(mask, p, 0.0)
        d = p * (dpt[:, part] - delta[:, part])
        probs.append(p.astype(jnp.bfloat16))
        dscores.append(d.astype(jnp.bfloat16))
    return jnp.concatenate(probs, axis=1), jnp.concatenate(dscores, axis=1)


def doc_start(pos, ends):
    begin = jnp.zeros_like(pos)
    for e in ends:
        begin = jnp.where(pos >= e, e, begin)
    return begin


def doc_ends(facts):
    e0 = facts[NBLK]
    e1 = e0 + facts[NBLK + 1]
    return e0, e1, e1 + facts[NBLK + 2]


def gather_kernel(
    facts_ref, q_ref, kv_ref, o_ref, do_ref, lse_ref,
    ks, vs, qs, dos, stats, lkv, l0, l1, l2, l3, l4,
    o_buf, do_buf, aux, auxx, nq, ndo, nkv, sq, sdo, skv, sstats, sacc, sdq, sj, ssem, rsem, hssem, hrsem, lsem,
):
    a, b, sa, sb = place()
    A = [lax.rem(a + t, SIDE) for t in range(SIDE)]
    B = [lax.rem(b + t, SIDE) for t in range(SIDE)]

    def dev(aa, bb):
        return {"seq": aa * sa + bb * sb}

    def slot(aa, bb):
        return span(aa * sa + bb * sb, ROWS)

    kvs = (ks, vs)
    ldq = (l0, l1, l2, l3, l4)

    def local(src, dst, n):
        copy = pltpu.make_async_copy(src, dst, lsem.at[n])
        copy.start()
        return copy

    loads = [local(o_ref, o_buf, 0), local(do_ref, do_buf, 1)]
    mine = slot(a, b)
    own_kv = [local(kv_ref.at[:, span(a + SIDE * n, HD)], kvs[n].at[mine], 2 + n) for n in range(2)]
    own_q = []
    for h in range(GROUP):
        for n, (s, d) in enumerate(((q_ref, qs), (do_ref, dos))):
            own_q.append(local(s.at[:, span(a * GROUP + h, HD)], d.at[a, h], 4 + 2 * h + n))
    greet([dev(A[1], b), dev(A[3], b), dev(A[2], b), dev(a, B[1]), dev(a, B[3])])
    wires = Wires(ssem, rsem)
    first = {}
    for t in (1, 3, 2):
        first[t] = [
            wires.send(kv_ref.at[:, span(A[t] + SIDE * n, HD)], kvs[n].at[mine], dev(A[t], b))
            for n in range(2)
        ]
    def head_copy(h, n, t):
        src, dst = ((q_ref, qs), (do_ref, dos))[n]
        sem = (h * 2 + n) * 3 + t - 1
        return pltpu.make_async_remote_copy(
            src.at[:, span(A[t] * GROUP + h, HD)], dst.at[a, h], hssem.at[sem], hrsem.at[sem],
            device_id=dev(A[t], b), device_id_type=MESH,
        )

    def send_head(h):
        for n in range(2):
            for t in (2, 1, 3):
                head_copy(h, n, t).start()

    for h in range(BEFORE):
        send_head(h)

    for load in loads:
        load.wait()
    ones = jnp.ones((8, HD), jnp.bfloat16)
    aux[...] = jnp.zeros_like(aux)
    for g in range(SIDE):
        for h in range(GROUP):
            n = g * GROUP + h
            cols = slice(n * HD, (n + 1) * HD)
            prod = o_buf[:, cols].astype(jnp.float32) * do_buf[:, cols].astype(jnp.float32)
            high = prod.astype(jnp.bfloat16)
            low = (prod - high.astype(jnp.float32)).astype(jnp.bfloat16)
            delta = lax.dot_general(ones, high, NT, preferred_element_type=jnp.float32)
            delta += lax.dot_general(ones, low, NT, preferred_element_type=jnp.float32)
            aux[g, h : h + 1, :] = lse_ref[n : n + 1, :] * LOG2E
            aux[g, 8 + h : 9 + h, :] = delta[0:1]
    facts = [wires.send(aux.at[A[t]], auxx.at[a], dev(A[t], b)) for t in (1, 3, 2)]
    own_q.append(local(aux.at[a], auxx.at[a], 14))
    for h in range(BEFORE, GROUP):
        send_head(h)

    passed = {}

    def spread(t):
        rows = slot(A[t], b)
        passed[t] = [[wires.send(x.at[rows], x.at[rows], dev(a, B[n])) for x in kvs] for n in (1, 3)]

    for copy in own_kv:
        copy.wait()
    spread(0)
    for t in (1, 3, 2):
        for copy in first[SIDE - t]:
            copy.wait_recv()
        spread(t)
    for copy in own_q + facts:
        copy.wait()
    for m in range(NLOC):
        tok = slice((m % 2) * BLK, (m % 2 + 1) * BLK)
        for h in range(GROUP):
            part = slice(h * BLK, (h + 1) * BLK)
            stats[m, 0:1, part] = auxx[m // 2, h : h + 1, tok]
            stats[m, 1:2, part] = auxx[m // 2, 8 + h : 9 + h, tok]

    order = facts_ref
    ends = doc_ends(order)
    js = [order[(m // 2 * sa + b * sb) * 2 + m % 2] for m in range(NLOC)]
    ranks = [
        sum((js[i] < js[m] if i > m else js[i] <= js[m]).astype(jnp.int32) for i in range(NLOC) if i != m)
        for m in range(NLOC)
    ]
    for m in range(NLOC):
        here = span((m // 2 * sa + b * sb) * 2 + m % 2, BLK)
        nkv[m] = jnp.concatenate([ks[here, :], vs[here, :]], axis=1)
    kinds = [sum(jnp.where(ranks[i] == r, i, 0) for i in range(NLOC)) for r in range(NLOC)]
    for r, m in enumerate(kinds):
        sj[r] = sum(jnp.where(ranks[i] == r, js[i], 0) for i in range(NLOC))
        skv[r * BLK : (r + 1) * BLK, :] = nkv[m]
        facts_r = stats[m]
        for h in range(GROUP):
            sstats[h, :, r * BLK : (r + 1) * BLK] = facts_r[:, h * BLK : (h + 1) * BLK]
    sacc[...] = jnp.zeros_like(sacc)
    iota = lax.broadcasted_iota(jnp.int32, (BLK, BLK), 0)
    kpos = [sj[r] * BLK + iota for r in range(NLOC)]
    qpos = [sj[r] * BLK + lax.broadcasted_iota(jnp.int32, (1, BLK), 1) for r in range(NLOC)]
    qbegin = [doc_start(pos, ends) for pos in qpos]

    second = {}

    def forward(t):
        up, down = passed[t]
        for copy in up if t < 2 else down:
            copy.wait_recv()
        rows = slot(A[t], B[3] if t < 2 else B[1])
        second[t] = [wires.send(x.at[rows], x.at[rows], dev(a, B[1] if t < 2 else B[3])) for x in kvs]

    def head(h, carry):
        for n in range(2):
            for t in (2, 1, 3):
                head_copy(h, n, t).wait_recv()
        for m in range(NLOC):
            half = slice(m % 2 * BLK, (m % 2 + 1) * BLK)
            nq[m] = qs[m // 2, h, half, :]
            ndo[m] = dos[m // 2, h, half, :]
        for r, m in enumerate(kinds):
            sq[r * BLK : (r + 1) * BLK, :] = nq[m]
            sdo[r * BLK : (r + 1) * BLK, :] = ndo[m]
        st = sstats[h]
        work = []
        for m in range(SIDE):
            keys = skv[0 : (m + 1) * PAIR, :]
            wide = slice(m * PAIR, (m + 1) * PAIR)
            q, do = sq[wide, :], sdo[wide, :]
            sc = lax.dot_general(keys[:, 0:HD], q, NT, preferred_element_type=jnp.float32)
            dp = lax.dot_general(keys[:, HD : 2 * HD], do, NT, preferred_element_type=jnp.float32)
            probs, dscores = [], []
            for u in range(2):
                r = 2 * m + u
                part = slice(u * BLK, (u + 1) * BLK)
                masks = [kpos[n] >= qbegin[r] for n in range(2 * m)]
                masks += [(kpos[n] >= qbegin[r]) & (kpos[n] <= qpos[r]) for n in (2 * m, 2 * m + 1)]
                tok = slice(r * BLK, (r + 1) * BLK)
                p = jnp.exp2(sc[:, part] * (SCALE * LOG2E) - st[0:1, tok])
                p = jnp.where(jnp.concatenate(masks), p, 0.0)
                d = p * (dp[:, part] - st[1:2, tok])
                probs.append(p.astype(jnp.bfloat16))
                dscores.append(d.astype(jnp.bfloat16))
            work.append((keys, q, do, jnp.concatenate(probs, axis=1), jnp.concatenate(dscores, axis=1)))
        for m, (keys, q, do, p, d) in enumerate(work):
            gv = jnp.dot(p, do, preferred_element_type=jnp.float32)
            gk = jnp.dot(d, q, preferred_element_type=jnp.float32)
            for r in range(2 * m + 2):
                rows = slice(r * BLK, (r + 1) * BLK)
                sacc[r, :, HD : 2 * HD] += gv[rows]
                sacc[r, :, 0:HD] += gk[rows]
            g = lax.dot_general(keys[:, 0:HD], d, TN, preferred_element_type=jnp.float32)
            for u in range(2):
                sdq[2 * m + u, h] = g[:, u * BLK : (u + 1) * BLK]
        return carry

    done = 0
    for t, upto in zip((0, 3, 1, 2), AT):
        if upto > done:
            lax.fori_loop(done, upto, head, 0)
            done = upto
        forward(t)
    lax.fori_loop(done, GROUP, head, 0)
    for m in range(NLOC):
        lkv[m] = sacc[ranks[m]]
        mine_dq = sdq[ranks[m]]
        for h in range(GROUP):
            ldq[h][m] = mine_dq[h]

    for t in range(SIDE):
        for copy in passed[t][1 if t < 2 else 0]:
            copy.wait_recv()
        for copy in second[t]:
            copy.wait()
        for copy in passed[t][0] + passed[t][1]:
            copy.wait_send()
    for t in (1, 3, 2):
        for copy in first[t]:
            copy.wait_send()
    for h in range(GROUP):
        for n in range(2):
            for t in (1, 2, 3):
                head_copy(h, n, t).wait_send()


def attend_kernel(order, ks, vs, qs, dos, stats, acc, dqt, inverse, jq, iq, ik, iodd, kodd):
    a, b, sa, sb = place()
    core = lax.rem(lax.axis_index("island"), 2)
    ends = doc_ends(order)

    def invert(n, carry):
        inverse[order[n]] = n
        return carry

    lax.fori_loop(0, NBLK, invert, 0, unroll=4)
    acc[...] = jnp.zeros_like(acc)
    dqt[...] = jnp.zeros_like(dqt)

    def plan(i, carry):
        p, odd = carry
        j = order[(i // 2 * sa + b * sb) * 2 + lax.rem(i, 2)]
        jq[i] = j
        low = doc_start(j * BLK, ends) // BLK

        def look(c, p):
            seq = inverse[c] // 2
            x, y = lax.rem(seq, SIDE), seq // SIDE
            ik[p] = c
            return p + (y + core * (x - y) != b).astype(jnp.int32)

        q = lax.fori_loop(low, j, look, p)
        rest = lax.rem(q, 2)
        iodd[odd] = i
        kodd[odd] = ik[jnp.maximum(q - 1, 0)]
        q = q - rest

        def name(t, carry):
            iq[t] = i
            return carry

        lax.fori_loop(p // 2, q // 2, name, 0)
        return q, odd + rest

    total, odd = lax.fori_loop(0, NLOC, plan, (0, 0))
    total = total // 2

    def front(t, size):
        i = iq[t] if size == 2 else iodd[t]
        c = [ik[2 * t + u] for u in range(2)] if size == 2 else [kodd[t]]
        at = [span(inverse[n], BLK) for n in c]
        keys = jnp.concatenate([ks[n, :] for n in at])
        values = jnp.concatenate([vs[n, :] for n in at])
        q = qs[i // 2, :, span(lax.rem(i, 2), BLK), :].reshape(QW, HD)
        do = dos[i // 2, :, span(lax.rem(i, 2), BLK), :].reshape(QW, HD)
        st = stats[i]
        pos = jq[i] * BLK + lax.broadcasted_iota(jnp.int32, (1, BLK), 1)
        iota = lax.broadcasted_iota(jnp.int32, (BLK, BLK), 0)
        mask = jnp.concatenate([n * BLK + iota for n in c]) >= doc_start(pos, ends)
        p, d = weigh(keys, values, q, do, st[0:1], st[1:2], mask)
        return i, at, keys, q, do, p, d

    def back(i, at, keys, q, do, p, d):
        gv = jnp.dot(p, do, preferred_element_type=jnp.float32)
        gk = jnp.dot(d, q, preferred_element_type=jnp.float32)
        for n in range(len(at)):
            acc[at[n], HD : 2 * HD] += gv[n * BLK : (n + 1) * BLK]
            acc[at[n], 0:HD] += gk[n * BLK : (n + 1) * BLK]
        dqt[i] += lax.dot_general(keys, d, TN, preferred_element_type=jnp.float32)

    def group(first, count, size):
        held = front(first, size)
        for u in range(1, count):
            following = front(first + u, size)
            back(*held)
            held = following
        back(*held)

    def run(total, deep, size):
        def many(s, carry):
            group(s * deep, deep, size)
            return carry

        def single(s, carry):
            group(s, 1, size)
            return carry

        lax.fori_loop(0, total // deep, many, 0)
        lax.fori_loop(total // deep * deep, total, single, 0)

    run(total, DEEP, 2)
    run(odd, 3, 1)


def scatter_kernel(
    acc, dqt, lkv, l0, l1, l2, l3, l4, dq, dk, dv, sent, mid, thr, got, grads, dqs, ssem, rsem, lsem
):
    a, b, sa, sb = place()
    A = [lax.rem(a + t, SIDE) for t in range(SIDE)]
    B = [lax.rem(b + t, SIDE) for t in range(SIDE)]

    def dev(aa, bb):
        return {"seq": aa * sa + bb * sb}

    up, down = dev(a, B[1]), dev(a, B[3])
    toward = (up, up, down, down)
    other = (down, down, up, up)
    next_b = (B[1], B[1], B[3], B[3])
    other_b = (B[3], B[3], B[1], B[1])

    def rows_of(bb, t, u):
        return acc[pl.ds(pl.multiple_of((A[t] * sa + bb * sb) * ROWS + u * BLK, BLK), BLK), :]

    order = [(t, u) for ts in ((2, 1), (3, 0)) for u in range(2) for t in ts]
    for t, u in order:
        sent[0, t, u] = rows_of(B[2], t, u).astype(jnp.bfloat16)
    greet([dev(A[1], b), dev(A[3], b), dev(A[2], b), up, down])
    wires = Wires(ssem, rsem)
    through, plain, summed = {}, {}, {}
    for t, u in order:
        through[t, u] = wires.send(sent.at[0, t, u], thr.at[t, u], toward[t])
    for t, u in order:
        sent[1, t, u] = rows_of(other_b[t], t, u).astype(jnp.bfloat16)
        plain[t, u] = wires.send(sent.at[1, t, u], got.at[1 if t < 2 else 0, t, u], other[t])

    heads, copies, last = [], [], []

    def give(t):
        for u in range(2):
            m = 2 * A[t] + u
            for h in range(GROUP):
                part = slice(h * BLK, (h + 1) * BLK)
                g = (dqt[m, :, part] + (l0, l1, l2, l3, l4)[h][m]) * SCALE
                dqs[t, u, :, part] = g.T.astype(jnp.bfloat16)
            dst = dq.at[pl.ds(u * BLK, BLK), span(a, QW)]
            if t:
                heads.append(wires.send(dqs.at[t, u], dst, dev(A[t], b)))
            else:
                copies.append(pltpu.make_async_copy(dqs.at[t, u], dst, lsem.at[u]))
                copies[-1].start()

    def pass_on(t, u):
        through[t, u].wait_recv()
        total = rows_of(next_b[t], t, u) + thr[t, u].astype(jnp.float32)
        mid[t, u] = total.astype(jnp.bfloat16)
        summed[t, u] = wires.send(mid.at[t, u], got.at[0 if t < 2 else 1, t, u], toward[t])

    give(2)
    give(1)
    for t, u in order[:4]:
        pass_on(t, u)
    give(3)
    for t, u in order[4:]:
        pass_on(t, u)
    give(0)
    for t, u in order:
        plain[t, u].wait_recv()
        summed[t, u].wait_recv()
        total = lkv[2 * A[t] + u] + got[0, t, u].astype(jnp.float32) + got[1, t, u].astype(jnp.float32)
        grads[t, u, :, 0:HD] = (total[:, 0:HD] * SCALE).astype(jnp.bfloat16)
        grads[t, u, :, HD : 2 * HD] = total[:, HD : 2 * HD].astype(jnp.bfloat16)
        for n, d in enumerate((dk, dv)):
            src = grads.at[t, u, :, pl.ds(n * HD, HD)]
            dst = d.at[pl.ds(u * BLK, BLK), span(a, HD)]
            if t:
                last.append(wires.send(src, dst, dev(A[t], b)))
            else:
                copies.append(pltpu.make_async_copy(src, dst, lsem.at[2 + 2 * u + n]))
                copies[-1].start()
    for copy in heads + last:
        copy.wait()
    for key in order:
        through[key].wait_send()
        plain[key].wait_send()
        summed[key].wait_send()
    for copy in copies:
        copy.wait()


def emit_kernel(*refs):
    sems = refs[-1]
    copies = [pltpu.make_async_copy(refs[n], refs[n + 3], sems.at[n]) for n in range(3)]
    for copy in copies:
        copy.start()
    for copy in copies:
        copy.wait()


ANY = pl.BlockSpec(memory_space=pl.ANY)
HBM = pl.BlockSpec(memory_space=pltpu.HBM)
VMEM = pl.BlockSpec(memory_space=pltpu.VMEM)
SMEM = pl.BlockSpec(memory_space=pltpu.SMEM)
BF = jnp.bfloat16
F32 = jnp.float32
MIB = 2**20


def shapes(*pairs):
    return [jax.ShapeDtypeStruct(s, d) for s, d in pairs]


def gather_call(facts, query, kv, attn_out, out_grad, log_sums):
    packed = (SIDE, GROUP, ROWS, HD)
    return pl.pallas_call(
        gather_kernel,
        out_shape=shapes(
            ((TOKENS, HD), BF), ((TOKENS, HD), BF), (packed, BF), (packed, BF), ((NLOC, 8, QW), F32),
            ((NLOC, BLK, 2 * HD), F32), *[((NLOC, HD, BLK), F32)] * GROUP,
        ),
        in_specs=[SMEM] + [HBM] * 4 + [VMEM],
        out_specs=[VMEM] * 11,
        scratch_shapes=[
            pltpu.VMEM((ROWS, SIDE * QW), BF),
            pltpu.VMEM((ROWS, SIDE * QW), BF),
            pltpu.VMEM((SIDE, 16, ROWS), F32),
            pltpu.VMEM((SIDE, 16, ROWS), F32),
            pltpu.VMEM((NLOC, BLK, HD), BF),
            pltpu.VMEM((NLOC, BLK, HD), BF),
            pltpu.VMEM((NLOC, BLK, 2 * HD), BF),
            pltpu.VMEM((NLOC * BLK, HD), BF),
            pltpu.VMEM((NLOC * BLK, HD), BF),
            pltpu.VMEM((NLOC * BLK, 2 * HD), BF),
            pltpu.VMEM((GROUP, 8, NLOC * BLK), F32),
            pltpu.VMEM((NLOC, BLK, 2 * HD), F32),
            pltpu.VMEM((NLOC, GROUP, HD, BLK), F32),
            pltpu.SMEM((NLOC,), jnp.int32),
            pltpu.SemaphoreType.DMA((40,)),
            pltpu.SemaphoreType.DMA((40,)),
            pltpu.SemaphoreType.DMA((30,)),
            pltpu.SemaphoreType.DMA((30,)),
            pltpu.SemaphoreType.DMA((16,)),
        ],
        compiler_params=pltpu.CompilerParams(
            collective_id=1, has_side_effects=True, vmem_limit_bytes=45 * MIB
        ),
        name="gather",
    )(facts, query, kv, attn_out, out_grad, log_sums)


def attend_call(facts, ks, vs, qs, dos, stats):
    return pl.pallas_call(
        attend_kernel,
        out_shape=shapes(((TOKENS, 2 * HD), F32), ((NLOC, HD, QW), F32)),
        in_specs=[SMEM] + [VMEM] * 5,
        out_specs=[VMEM, VMEM],
        scratch_shapes=[
            pltpu.SMEM((NBLK,), jnp.int32),
            pltpu.SMEM((NLOC,), jnp.int32),
            pltpu.SMEM((128,), jnp.int32),
            pltpu.SMEM((256,), jnp.int32),
            pltpu.SMEM((2 * NLOC,), jnp.int32),
            pltpu.SMEM((2 * NLOC,), jnp.int32),
        ],
        compiler_params=pltpu.CompilerParams(vmem_limit_bytes=28 * MIB),
        name="attend",
    )(facts, ks, vs, qs, dos, stats)


def scatter_call(acc, dqt, lkv, *ldq):
    piece = (SIDE, 2, BLK, 2 * HD)
    return pl.pallas_call(
        scatter_kernel,
        out_shape=shapes(((ROWS, SIDE * QW), BF), ((ROWS, SIDE * HD), BF), ((ROWS, SIDE * HD), BF)),
        in_specs=[VMEM] * 8,
        out_specs=[ANY] * 3,
        scratch_shapes=[
            pltpu.VMEM((2,) + piece, BF),
            pltpu.VMEM(piece, BF),
            pltpu.VMEM(piece, BF),
            pltpu.VMEM((2,) + piece, BF),
            pltpu.VMEM(piece, BF),
            pltpu.VMEM((SIDE, 2, BLK, QW), BF),
            pltpu.SemaphoreType.DMA((48,)),
            pltpu.SemaphoreType.DMA((48,)),
            pltpu.SemaphoreType.DMA((8,)),
        ],
        compiler_params=pltpu.CompilerParams(
            collective_id=2, has_side_effects=True, vmem_limit_bytes=28 * MIB
        ),
        name="scatter",
    )(acc, dqt, lkv, *ldq)


def emit_call(*grads):
    return pl.pallas_call(
        emit_kernel,
        out_shape=shapes(*((g.shape, g.dtype) for g in grads)),
        in_specs=[VMEM] * 3,
        out_specs=[HBM] * 3,
        scratch_shapes=[pltpu.SemaphoreType.DMA((3,))],
        compiler_params=pltpu.CompilerParams(vmem_limit_bytes=4 * MIB),
        name="emit",
    )(*grads)


def body(query, key, value, attn_out, out_grad, log_sums, block_order, doc_lengths):
    facts = jnp.concatenate([block_order, doc_lengths])
    kv = jnp.concatenate([key, value], axis=1)
    ks, vs, qs, dos, stats, lkv, *ldq = gather_call(facts, query, kv, attn_out, out_grad, log_sums)
    acc, dqt = attend_call(facts, ks, vs, qs, dos, stats)
    return emit_call(*scatter_call(acc, dqt, lkv, *ldq))


def solution(mesh):
    rows = P(("island", "seq"), None)
    return jax.shard_map(
        body,
        mesh=mesh,
        in_specs=(rows,) * 5 + (P(None, ("island", "seq")), P("island"), P("island")),
        out_specs=(rows,) * 3,
        check_vma=False,
    )
```

```python
import functools
import math

import jax
import jax.numpy as jnp
from jax import lax
from jax.experimental import pallas as pl
from jax.experimental.pallas import tpu as pltpu
from jax.sharding import PartitionSpec as P

MESH = pl.DeviceIdType.MESH
HD = 128
BLK = 128
SIDE = 4
ROWS = 256
GROUP = 5
QW = GROUP * HD
TOKENS = 4096
MOST = 2048
NBLK = 32
PAIR = 2 * BLK
NLOC = 2 * SIDE
SCALE = 1.0 / math.sqrt(HD)
LOG2E = math.log2(math.e)
DEEP = 4
BEFORE = 1
AT = (1, 2, 3, 4)
NT = (((1,), (1,)), ((), ()))
TN = (((0,), (0,)), ((), ()))


def place():
    core = lax.rem(lax.axis_index("island"), 2)
    seq = lax.axis_index("seq")
    x, y = lax.rem(seq, SIDE), seq // SIDE
    a = x + core * (y - x)
    b = y + core * (x - y)
    return a, b, 1 + 3 * core, SIDE - 3 * core


class Wires:
    def __init__(self, send_sems, recv_sems):
        self.send_sems, self.recv_sems, self.count = send_sems, recv_sems, 0

    def send(self, src, dst, device):
        n = self.count
        self.count += 1
        copy = pltpu.make_async_remote_copy(
            src, dst, self.send_sems.at[n], self.recv_sems.at[n], device_id=device, device_id_type=MESH
        )
        copy.start()
        return copy


def span(start, size):
    return pl.ds(pl.multiple_of(start * size, size), size)


def greet(devices):
    barrier = pltpu.get_barrier_semaphore()
    for device in devices:
        pl.semaphore_signal(barrier, inc=1, device_id=device, device_id_type=MESH)
    pl.semaphore_wait(barrier, len(devices))


def weigh(keys, values, q, do, lse, delta, mask):
    st = lax.dot_general(keys, q, NT, preferred_element_type=jnp.float32)
    dpt = lax.dot_general(values, do, NT, preferred_element_type=jnp.float32)
    probs, dscores = [], []
    for n in range(q.shape[0] // BLK):
        part = slice(n * BLK, (n + 1) * BLK)
        p = jnp.exp2(st[:, part] * (SCALE * LOG2E) - lse[:, part])
        p = jnp.where(mask, p, 0.0)
        d = p * (dpt[:, part] - delta[:, part])
        probs.append(p.astype(jnp.bfloat16))
        dscores.append(d.astype(jnp.bfloat16))
    return jnp.concatenate(probs, axis=1), jnp.concatenate(dscores, axis=1)


def doc_start(pos, ends):
    begin = jnp.zeros_like(pos)
    for e in ends:
        begin = jnp.where(pos >= e, e, begin)
    return begin


def doc_ends(facts):
    e0 = facts[NBLK]
    e1 = e0 + facts[NBLK + 1]
    return e0, e1, e1 + facts[NBLK + 2]


def gather_kernel(
    facts_ref, q_ref, kv_ref, o_ref, do_ref, lse_ref,
    ks, vs, qs, dos, stats, lkv, l0, l1, l2, l3, l4,
    o_buf, do_buf, aux, auxx, nq, ndo, nkv, sq, sdo, skv, sstats, sacc, sdq, sj, ssem, rsem, hssem, hrsem, lsem,
):
    a, b, sa, sb = place()
    A = [lax.rem(a + t, SIDE) for t in range(SIDE)]
    B = [lax.rem(b + t, SIDE) for t in range(SIDE)]

    def dev(aa, bb):
        return {"seq": aa * sa + bb * sb}

    def slot(aa, bb):
        return span(aa * sa + bb * sb, ROWS)

    kvs = (ks, vs)
    ldq = (l0, l1, l2, l3, l4)

    def local(src, dst, n):
        copy = pltpu.make_async_copy(src, dst, lsem.at[n])
        copy.start()
        return copy

    loads = [local(o_ref, o_buf, 0), local(do_ref, do_buf, 1)]
    mine = slot(a, b)
    own_kv = [local(kv_ref.at[:, span(a + SIDE * n, HD)], kvs[n].at[mine], 2 + n) for n in range(2)]
    own_q = []
    for h in range(GROUP):
        for n, (s, d) in enumerate(((q_ref, qs), (do_ref, dos))):
            own_q.append(local(s.at[:, span(a * GROUP + h, HD)], d.at[a, h], 4 + 2 * h + n))
    greet([dev(A[1], b), dev(A[3], b), dev(A[2], b), dev(a, B[1]), dev(a, B[3])])
    wires = Wires(ssem, rsem)
    first = {}
    for t in (1, 3, 2):
        first[t] = [
            wires.send(kv_ref.at[:, span(A[t] + SIDE * n, HD)], kvs[n].at[mine], dev(A[t], b))
            for n in range(2)
        ]
    def head_copy(h, n, t):
        src, dst = ((q_ref, qs), (do_ref, dos))[n]
        sem = (h * 2 + n) * 3 + t - 1
        return pltpu.make_async_remote_copy(
            src.at[:, span(A[t] * GROUP + h, HD)], dst.at[a, h], hssem.at[sem], hrsem.at[sem],
            device_id=dev(A[t], b), device_id_type=MESH,
        )

    def send_head(h):
        for n in range(2):
            for t in (2, 1, 3):
                head_copy(h, n, t).start()

    for h in range(BEFORE):
        send_head(h)

    for load in loads:
        load.wait()
    ones = jnp.ones((8, HD), jnp.bfloat16)
    aux[...] = jnp.zeros_like(aux)
    for g in range(SIDE):
        for h in range(GROUP):
            n = g * GROUP + h
            cols = slice(n * HD, (n + 1) * HD)
            prod = o_buf[:, cols].astype(jnp.float32) * do_buf[:, cols].astype(jnp.float32)
            high = prod.astype(jnp.bfloat16)
            low = (prod - high.astype(jnp.float32)).astype(jnp.bfloat16)
            delta = lax.dot_general(ones, high, NT, preferred_element_type=jnp.float32)
            delta += lax.dot_general(ones, low, NT, preferred_element_type=jnp.float32)
            aux[g, h : h + 1, :] = lse_ref[n : n + 1, :] * LOG2E
            aux[g, 8 + h : 9 + h, :] = delta[0:1]
    facts = [wires.send(aux.at[A[t]], auxx.at[a], dev(A[t], b)) for t in (1, 3, 2)]
    own_q.append(local(aux.at[a], auxx.at[a], 14))
    for h in range(BEFORE, GROUP):
        send_head(h)

    passed = {}

    def spread(t):
        rows = slot(A[t], b)
        passed[t] = [[wires.send(x.at[rows], x.at[rows], dev(a, B[n])) for x in kvs] for n in (1, 3)]

    for copy in own_kv:
        copy.wait()
    spread(0)
    for t in (1, 3, 2):
        for copy in first[SIDE - t]:
            copy.wait_recv()
        spread(t)
    for copy in own_q + facts:
        copy.wait()
    for m in range(NLOC):
        tok = slice((m % 2) * BLK, (m % 2 + 1) * BLK)
        for h in range(GROUP):
            part = slice(h * BLK, (h + 1) * BLK)
            stats[m, 0:1, part] = auxx[m // 2, h : h + 1, tok]
            stats[m, 1:2, part] = auxx[m // 2, 8 + h : 9 + h, tok]

    order = facts_ref
    ends = doc_ends(order)
    js = [order[(m // 2 * sa + b * sb) * 2 + m % 2] for m in range(NLOC)]
    ranks = [
        sum((js[i] < js[m] if i > m else js[i] <= js[m]).astype(jnp.int32) for i in range(NLOC) if i != m)
        for m in range(NLOC)
    ]
    for m in range(NLOC):
        here = span((m // 2 * sa + b * sb) * 2 + m % 2, BLK)
        nkv[m] = jnp.concatenate([ks[here, :], vs[here, :]], axis=1)
    kinds = [sum(jnp.where(ranks[i] == r, i, 0) for i in range(NLOC)) for r in range(NLOC)]
    for r, m in enumerate(kinds):
        sj[r] = sum(jnp.where(ranks[i] == r, js[i], 0) for i in range(NLOC))
        skv[r * BLK : (r + 1) * BLK, :] = nkv[m]
        facts_r = stats[m]
        for h in range(GROUP):
            sstats[h, :, r * BLK : (r + 1) * BLK] = facts_r[:, h * BLK : (h + 1) * BLK]
    sacc[...] = jnp.zeros_like(sacc)
    iota = lax.broadcasted_iota(jnp.int32, (BLK, BLK), 0)
    kpos = [sj[r] * BLK + iota for r in range(NLOC)]
    qpos = [sj[r] * BLK + lax.broadcasted_iota(jnp.int32, (1, BLK), 1) for r in range(NLOC)]
    qbegin = [doc_start(pos, ends) for pos in qpos]

    second = {}

    def forward(t):
        up, down = passed[t]
        for copy in up if t < 2 else down:
            copy.wait_recv()
        rows = slot(A[t], B[3] if t < 2 else B[1])
        second[t] = [wires.send(x.at[rows], x.at[rows], dev(a, B[1] if t < 2 else B[3])) for x in kvs]

    def head(h, carry):
        for n in range(2):
            for t in (2, 1, 3):
                head_copy(h, n, t).wait_recv()
        for m in range(NLOC):
            half = slice(m % 2 * BLK, (m % 2 + 1) * BLK)
            nq[m] = qs[m // 2, h, half, :]
            ndo[m] = dos[m // 2, h, half, :]
        for r, m in enumerate(kinds):
            sq[r * BLK : (r + 1) * BLK, :] = nq[m]
            sdo[r * BLK : (r + 1) * BLK, :] = ndo[m]
        st = sstats[h]
        work = []
        for m in range(SIDE):
            keys = skv[0 : (m + 1) * PAIR, :]
            wide = slice(m * PAIR, (m + 1) * PAIR)
            q, do = sq[wide, :], sdo[wide, :]
            sc = lax.dot_general(keys[:, 0:HD], q, NT, preferred_element_type=jnp.float32)
            dp = lax.dot_general(keys[:, HD : 2 * HD], do, NT, preferred_element_type=jnp.float32)
            probs, dscores = [], []
            for u in range(2):
                r = 2 * m + u
                part = slice(u * BLK, (u + 1) * BLK)
                masks = [kpos[n] >= qbegin[r] for n in range(2 * m)]
                masks += [(kpos[n] >= qbegin[r]) & (kpos[n] <= qpos[r]) for n in (2 * m, 2 * m + 1)]
                tok = slice(r * BLK, (r + 1) * BLK)
                p = jnp.exp2(sc[:, part] * (SCALE * LOG2E) - st[0:1, tok])
                p = jnp.where(jnp.concatenate(masks), p, 0.0)
                d = p * (dp[:, part] - st[1:2, tok])
                probs.append(p.astype(jnp.bfloat16))
                dscores.append(d.astype(jnp.bfloat16))
            work.append((keys, q, do, jnp.concatenate(probs, axis=1), jnp.concatenate(dscores, axis=1)))
        for m, (keys, q, do, p, d) in enumerate(work):
            gv = jnp.dot(p, do, preferred_element_type=jnp.float32)
            gk = jnp.dot(d, q, preferred_element_type=jnp.float32)
            for r in range(2 * m + 2):
                rows = slice(r * BLK, (r + 1) * BLK)
                sacc[r, :, HD : 2 * HD] += gv[rows]
                sacc[r, :, 0:HD] += gk[rows]
            g = lax.dot_general(keys[:, 0:HD], d, TN, preferred_element_type=jnp.float32)
            for u in range(2):
                sdq[2 * m + u, h] = g[:, u * BLK : (u + 1) * BLK]
        return carry

    done = 0
    for t, upto in zip((0, 3, 1, 2), AT):
        if upto > done:
            lax.fori_loop(done, upto, head, 0)
            done = upto
        forward(t)
    lax.fori_loop(done, GROUP, head, 0)
    for m in range(NLOC):
        lkv[m] = sacc[ranks[m]]
        mine_dq = sdq[ranks[m]]
        for h in range(GROUP):
            ldq[h][m] = mine_dq[h]

    for t in range(SIDE):
        for copy in passed[t][1 if t < 2 else 0]:
            copy.wait_recv()
        for copy in second[t]:
            copy.wait()
        for copy in passed[t][0] + passed[t][1]:
            copy.wait_send()
    for t in (1, 3, 2):
        for copy in first[t]:
            copy.wait_send()
    for h in range(GROUP):
        for n in range(2):
            for t in (1, 2, 3):
                head_copy(h, n, t).wait_send()


def attend_kernel(order, ks, vs, qs, dos, stats, acc, dqt, inverse, far, jq, iq, ik, iodd, kodd):
    a, b, sa, sb = place()
    core = lax.rem(lax.axis_index("island"), 2)
    ends = doc_ends(order)

    for n in range(NBLK):
        x, y = n // 2 % SIDE, n // 2 // SIDE
        inverse[order[n]] = n
        far[order[n]] = (y + core * (x - y) != b).astype(jnp.int32)
    def plan(i, carry):
        p, odd = carry
        acc[span(i, TOKENS // NLOC), :] = jnp.zeros((TOKENS // NLOC, 2 * HD), jnp.float32)
        dqt[i] = jnp.zeros((HD, QW), jnp.float32)
        j = order[(i // 2 * sa + b * sb) * 2 + lax.rem(i, 2)]
        jq[i] = j
        low = doc_start(j * BLK, ends) // BLK

        q = p
        for n in range(1, MOST // BLK + 1):
            c = jnp.maximum(j - n, 0)
            ik[q] = c
            q = q + jnp.where(j - n >= low, far[c], 0)
        rest = lax.rem(q, 2)
        iodd[odd] = i
        kodd[odd] = ik[jnp.maximum(q - 1, 0)]
        q = q - rest

        def name(t, carry):
            iq[t] = i
            return carry

        lax.fori_loop(p // 2, q // 2, name, 0)
        return q, odd + rest

    total, odd = lax.fori_loop(0, NLOC, plan, (0, 0))
    total = total // 2

    def front(t, size):
        i = iq[t] if size == 2 else iodd[t]
        c = [ik[2 * t + u] for u in range(2)] if size == 2 else [kodd[t]]
        at = [span(inverse[n], BLK) for n in c]
        keys = jnp.concatenate([ks[n, :] for n in at])
        values = jnp.concatenate([vs[n, :] for n in at])
        q = qs[i // 2, :, span(lax.rem(i, 2), BLK), :].reshape(QW, HD)
        do = dos[i // 2, :, span(lax.rem(i, 2), BLK), :].reshape(QW, HD)
        st = stats[i]
        pos = jq[i] * BLK + lax.broadcasted_iota(jnp.int32, (1, BLK), 1)
        iota = lax.broadcasted_iota(jnp.int32, (BLK, BLK), 0)
        mask = jnp.concatenate([n * BLK + iota for n in c]) >= doc_start(pos, ends)
        p, d = weigh(keys, values, q, do, st[0:1], st[1:2], mask)
        return i, at, keys, q, do, p, d

    def back(i, at, keys, q, do, p, d):
        gv = jnp.dot(p, do, preferred_element_type=jnp.float32)
        gk = jnp.dot(d, q, preferred_element_type=jnp.float32)
        for n in range(len(at)):
            acc[at[n], HD : 2 * HD] += gv[n * BLK : (n + 1) * BLK]
            acc[at[n], 0:HD] += gk[n * BLK : (n + 1) * BLK]
        dqt[i] += lax.dot_general(keys, d, TN, preferred_element_type=jnp.float32)

    def group(first, count, size):
        held = front(first, size)
        for u in range(1, count):
            following = front(first + u, size)
            back(*held)
            held = following
        back(*held)

    def run(total, deep, size):
        def many(s, carry):
            group(s * deep, deep, size)
            return carry

        def single(s, carry):
            group(s, 1, size)
            return carry

        lax.fori_loop(0, total // deep, many, 0)
        lax.fori_loop(total // deep * deep, total, single, 0)

    run(total, DEEP, 2)
    run(odd, 3, 1)


def scatter_kernel(
    acc, dqt, lkv, l0, l1, l2, l3, l4, dq, dk, dv, sent, mid, thr, got, grads, dqs, ssem, rsem, lsem
):
    a, b, sa, sb = place()
    A = [lax.rem(a + t, SIDE) for t in range(SIDE)]
    B = [lax.rem(b + t, SIDE) for t in range(SIDE)]

    def dev(aa, bb):
        return {"seq": aa * sa + bb * sb}

    up, down = dev(a, B[1]), dev(a, B[3])
    toward = (up, up, down, down)
    other = (down, down, up, up)
    next_b = (B[1], B[1], B[3], B[3])
    other_b = (B[3], B[3], B[1], B[1])

    def rows_of(bb, t, u):
        return acc[pl.ds(pl.multiple_of((A[t] * sa + bb * sb) * ROWS + u * BLK, BLK), BLK), :]

    order = [(t, u) for ts in ((2, 1), (3, 0)) for u in range(2) for t in ts]
    for t, u in order:
        sent[0, t, u] = rows_of(B[2], t, u).astype(jnp.bfloat16)
    greet([dev(A[1], b), dev(A[3], b), dev(A[2], b), up, down])
    wires = Wires(ssem, rsem)
    through, plain, summed = {}, {}, {}
    for t, u in order:
        through[t, u] = wires.send(sent.at[0, t, u], thr.at[t, u], toward[t])
    for t, u in order:
        sent[1, t, u] = rows_of(other_b[t], t, u).astype(jnp.bfloat16)
        plain[t, u] = wires.send(sent.at[1, t, u], got.at[1 if t < 2 else 0, t, u], other[t])

    heads, copies, last = [], [], []

    def give(t):
        for u in range(2):
            m = 2 * A[t] + u
            for h in range(GROUP):
                part = slice(h * BLK, (h + 1) * BLK)
                g = (dqt[m, :, part] + (l0, l1, l2, l3, l4)[h][m]) * SCALE
                dqs[t, u, :, part] = g.T.astype(jnp.bfloat16)
            dst = dq.at[pl.ds(u * BLK, BLK), span(a, QW)]
            if t:
                heads.append(wires.send(dqs.at[t, u], dst, dev(A[t], b)))
            else:
                copies.append(pltpu.make_async_copy(dqs.at[t, u], dst, lsem.at[u]))
                copies[-1].start()

    def pass_on(t, u):
        through[t, u].wait_recv()
        total = rows_of(next_b[t], t, u) + thr[t, u].astype(jnp.float32)
        mid[t, u] = total.astype(jnp.bfloat16)
        summed[t, u] = wires.send(mid.at[t, u], got.at[0 if t < 2 else 1, t, u], toward[t])

    give(2)
    give(1)
    for t, u in order[:4]:
        pass_on(t, u)
    give(3)
    for t, u in order[4:]:
        pass_on(t, u)
    give(0)
    for t, u in order:
        plain[t, u].wait_recv()
        summed[t, u].wait_recv()
        total = lkv[2 * A[t] + u] + got[0, t, u].astype(jnp.float32) + got[1, t, u].astype(jnp.float32)
        grads[t, u, :, 0:HD] = (total[:, 0:HD] * SCALE).astype(jnp.bfloat16)
        grads[t, u, :, HD : 2 * HD] = total[:, HD : 2 * HD].astype(jnp.bfloat16)
        for n, d in enumerate((dk, dv)):
            src = grads.at[t, u, :, pl.ds(n * HD, HD)]
            dst = d.at[pl.ds(u * BLK, BLK), span(a, HD)]
            if t:
                last.append(wires.send(src, dst, dev(A[t], b)))
            else:
                copies.append(pltpu.make_async_copy(src, dst, lsem.at[2 + 2 * u + n]))
                copies[-1].start()
    for copy in heads + last:
        copy.wait()
    for key in order:
        through[key].wait_send()
        plain[key].wait_send()
        summed[key].wait_send()
    for copy in copies:
        copy.wait()


def emit_kernel(*refs):
    sems = refs[-1]
    copies = [pltpu.make_async_copy(refs[n], refs[n + 3], sems.at[n]) for n in range(3)]
    for copy in copies:
        copy.start()
    for copy in copies:
        copy.wait()


ANY = pl.BlockSpec(memory_space=pl.ANY)
HBM = pl.BlockSpec(memory_space=pltpu.HBM)
VMEM = pl.BlockSpec(memory_space=pltpu.VMEM)
SMEM = pl.BlockSpec(memory_space=pltpu.SMEM)
BF = jnp.bfloat16
F32 = jnp.float32
MIB = 2**20


def shapes(*pairs):
    return [jax.ShapeDtypeStruct(s, d) for s, d in pairs]


def gather_call(facts, query, kv, attn_out, out_grad, log_sums):
    packed = (SIDE, GROUP, ROWS, HD)
    return pl.pallas_call(
        gather_kernel,
        out_shape=shapes(
            ((TOKENS, HD), BF), ((TOKENS, HD), BF), (packed, BF), (packed, BF), ((NLOC, 8, QW), F32),
            ((NLOC, BLK, 2 * HD), F32), *[((NLOC, HD, BLK), F32)] * GROUP,
        ),
        in_specs=[SMEM] + [HBM] * 4 + [VMEM],
        out_specs=[VMEM] * 11,
        scratch_shapes=[
            pltpu.VMEM((ROWS, SIDE * QW), BF),
            pltpu.VMEM((ROWS, SIDE * QW), BF),
            pltpu.VMEM((SIDE, 16, ROWS), F32),
            pltpu.VMEM((SIDE, 16, ROWS), F32),
            pltpu.VMEM((NLOC, BLK, HD), BF),
            pltpu.VMEM((NLOC, BLK, HD), BF),
            pltpu.VMEM((NLOC, BLK, 2 * HD), BF),
            pltpu.VMEM((NLOC * BLK, HD), BF),
            pltpu.VMEM((NLOC * BLK, HD), BF),
            pltpu.VMEM((NLOC * BLK, 2 * HD), BF),
            pltpu.VMEM((GROUP, 8, NLOC * BLK), F32),
            pltpu.VMEM((NLOC, BLK, 2 * HD), F32),
            pltpu.VMEM((NLOC, GROUP, HD, BLK), F32),
            pltpu.SMEM((NLOC,), jnp.int32),
            pltpu.SemaphoreType.DMA((40,)),
            pltpu.SemaphoreType.DMA((40,)),
            pltpu.SemaphoreType.DMA((30,)),
            pltpu.SemaphoreType.DMA((30,)),
            pltpu.SemaphoreType.DMA((16,)),
        ],
        compiler_params=pltpu.CompilerParams(
            collective_id=1, has_side_effects=True, vmem_limit_bytes=45 * MIB
        ),
        name="gather",
    )(facts, query, kv, attn_out, out_grad, log_sums)


def attend_call(facts, ks, vs, qs, dos, stats):
    return pl.pallas_call(
        attend_kernel,
        out_shape=shapes(((TOKENS, 2 * HD), F32), ((NLOC, HD, QW), F32)),
        in_specs=[SMEM] + [VMEM] * 5,
        out_specs=[VMEM, VMEM],
        scratch_shapes=[
            pltpu.SMEM((NBLK,), jnp.int32),
            pltpu.SMEM((NBLK,), jnp.int32),
            pltpu.SMEM((NLOC,), jnp.int32),
            pltpu.SMEM((128,), jnp.int32),
            pltpu.SMEM((256,), jnp.int32),
            pltpu.SMEM((2 * NLOC,), jnp.int32),
            pltpu.SMEM((2 * NLOC,), jnp.int32),
        ],
        compiler_params=pltpu.CompilerParams(vmem_limit_bytes=28 * MIB),
        name="attend",
    )(facts, ks, vs, qs, dos, stats)


def scatter_call(acc, dqt, lkv, *ldq):
    piece = (SIDE, 2, BLK, 2 * HD)
    return pl.pallas_call(
        scatter_kernel,
        out_shape=shapes(((ROWS, SIDE * QW), BF), ((ROWS, SIDE * HD), BF), ((ROWS, SIDE * HD), BF)),
        in_specs=[VMEM] * 8,
        out_specs=[ANY] * 3,
        scratch_shapes=[
            pltpu.VMEM((2,) + piece, BF),
            pltpu.VMEM(piece, BF),
            pltpu.VMEM(piece, BF),
            pltpu.VMEM((2,) + piece, BF),
            pltpu.VMEM(piece, BF),
            pltpu.VMEM((SIDE, 2, BLK, QW), BF),
            pltpu.SemaphoreType.DMA((48,)),
            pltpu.SemaphoreType.DMA((48,)),
            pltpu.SemaphoreType.DMA((8,)),
        ],
        compiler_params=pltpu.CompilerParams(
            collective_id=2, has_side_effects=True, vmem_limit_bytes=28 * MIB
        ),
        name="scatter",
    )(acc, dqt, lkv, *ldq)


def emit_call(*grads):
    return pl.pallas_call(
        emit_kernel,
        out_shape=shapes(*((g.shape, g.dtype) for g in grads)),
        in_specs=[VMEM] * 3,
        out_specs=[HBM] * 3,
        scratch_shapes=[pltpu.SemaphoreType.DMA((3,))],
        compiler_params=pltpu.CompilerParams(vmem_limit_bytes=4 * MIB),
        name="emit",
    )(*grads)


def body(query, key, value, attn_out, out_grad, log_sums, block_order, doc_lengths):
    facts = jnp.concatenate([block_order, doc_lengths])
    kv = jnp.concatenate([key, value], axis=1)
    ks, vs, qs, dos, stats, lkv, *ldq = gather_call(facts, query, kv, attn_out, out_grad, log_sums)
    acc, dqt = attend_call(facts, ks, vs, qs, dos, stats)
    return emit_call(*scatter_call(acc, dqt, lkv, *ldq))


def solution(mesh):
    rows = P(("island", "seq"), None)
    return jax.shard_map(
        body,
        mesh=mesh,
        in_specs=(rows,) * 5 + (P(None, ("island", "seq")), P("island"), P("island")),
        out_specs=(rows,) * 3,
        check_vma=False,
    )
```

```python
import functools
import math

import jax
import jax.numpy as jnp
from jax import lax
from jax.experimental import pallas as pl
from jax.experimental.pallas import tpu as pltpu
from jax.sharding import PartitionSpec as P

MESH = pl.DeviceIdType.MESH
HD = 128
BLK = 128
SIDE = 4
ROWS = 256
GROUP = 5
QW = GROUP * HD
TOKENS = 4096
MOST = 2048
NBLK = 32
PAIR = 2 * BLK
NLOC = 2 * SIDE
SCALE = 1.0 / math.sqrt(HD)
LOG2E = math.log2(math.e)
DEEP = 4
BEFORE = 1
AT = (1, 2, 3, 4)
NT = (((1,), (1,)), ((), ()))
TN = (((0,), (0,)), ((), ()))


def place():
    core = lax.rem(lax.axis_index("island"), 2)
    seq = lax.axis_index("seq")
    x, y = lax.rem(seq, SIDE), seq // SIDE
    a = x + core * (y - x)
    b = y + core * (x - y)
    return a, b, 1 + 3 * core, SIDE - 3 * core


class Wires:
    def __init__(self, send_sems, recv_sems):
        self.send_sems, self.recv_sems, self.count = send_sems, recv_sems, 0

    def send(self, src, dst, device):
        n = self.count
        self.count += 1
        copy = pltpu.make_async_remote_copy(
            src, dst, self.send_sems.at[n], self.recv_sems.at[n], device_id=device, device_id_type=MESH
        )
        copy.start()
        return copy


def span(start, size):
    return pl.ds(pl.multiple_of(start * size, size), size)


def greet(devices):
    barrier = pltpu.get_barrier_semaphore()
    for device in devices:
        pl.semaphore_signal(barrier, inc=1, device_id=device, device_id_type=MESH)
    pl.semaphore_wait(barrier, len(devices))


def weigh(keys, values, q, do, lse, delta, mask):
    st = lax.dot_general(keys, q, NT, preferred_element_type=jnp.float32)
    dpt = lax.dot_general(values, do, NT, preferred_element_type=jnp.float32)
    probs, dscores = [], []
    for n in range(q.shape[0] // BLK):
        part = slice(n * BLK, (n + 1) * BLK)
        p = jnp.exp2(st[:, part] * (SCALE * LOG2E) - lse[:, part])
        p = jnp.where(mask, p, 0.0)
        d = p * (dpt[:, part] - delta[:, part])
        probs.append(p.astype(jnp.bfloat16))
        dscores.append(d.astype(jnp.bfloat16))
    return jnp.concatenate(probs, axis=1), jnp.concatenate(dscores, axis=1)


def doc_start(pos, ends):
    begin = jnp.zeros_like(pos)
    for e in ends:
        begin = jnp.where(pos >= e, e, begin)
    return begin


def doc_ends(facts):
    e0 = facts[NBLK]
    e1 = e0 + facts[NBLK + 1]
    return e0, e1, e1 + facts[NBLK + 2]


def gather_kernel(
    facts_ref, q_ref, kv_ref, o_ref, do_ref, lse_ref,
    ks, vs, qs, dos, stats, lkv, l0, l1, l2, l3, l4,
    o_buf, do_buf, aux, auxx, nq, ndo, nkv, sq, sdo, skv, sstats, sacc, sdq, sj, ssem, rsem, hssem, hrsem, lsem,
):
    a, b, sa, sb = place()
    A = [lax.rem(a + t, SIDE) for t in range(SIDE)]
    B = [lax.rem(b + t, SIDE) for t in range(SIDE)]

    def dev(aa, bb):
        return {"seq": aa * sa + bb * sb}

    def slot(aa, bb):
        return span(aa * sa + bb * sb, ROWS)

    kvs = (ks, vs)
    ldq = (l0, l1, l2, l3, l4)

    def local(src, dst, n):
        copy = pltpu.make_async_copy(src, dst, lsem.at[n])
        copy.start()
        return copy

    loads = [local(o_ref, o_buf, 0), local(do_ref, do_buf, 1)]
    mine = slot(a, b)
    own_kv = [local(kv_ref.at[:, span(a + SIDE * n, HD)], kvs[n].at[mine], 2 + n) for n in range(2)]
    own_q = []
    for h in range(GROUP):
        for n, (s, d) in enumerate(((q_ref, qs), (do_ref, dos))):
            own_q.append(local(s.at[:, span(a * GROUP + h, HD)], d.at[a, h], 4 + 2 * h + n))
    greet([dev(A[1], b), dev(A[3], b), dev(A[2], b), dev(a, B[1]), dev(a, B[3])])
    wires = Wires(ssem, rsem)
    first = {}
    for t in (1, 3, 2):
        first[t] = [
            wires.send(kv_ref.at[:, span(A[t] + SIDE * n, HD)], kvs[n].at[mine], dev(A[t], b))
            for n in range(2)
        ]
    def head_copy(h, n, t):
        src, dst = ((q_ref, qs), (do_ref, dos))[n]
        sem = (h * 2 + n) * 3 + t - 1
        return pltpu.make_async_remote_copy(
            src.at[:, span(A[t] * GROUP + h, HD)], dst.at[a, h], hssem.at[sem], hrsem.at[sem],
            device_id=dev(A[t], b), device_id_type=MESH,
        )

    def send_head(h):
        for n in range(2):
            for t in (2, 1, 3):
                head_copy(h, n, t).start()

    for h in range(BEFORE):
        send_head(h)

    for load in loads:
        load.wait()
    ones = jnp.ones((8, HD), jnp.bfloat16)
    aux[...] = jnp.zeros_like(aux)
    for g in range(SIDE):
        for h in range(GROUP):
            n = g * GROUP + h
            cols = slice(n * HD, (n + 1) * HD)
            prod = o_buf[:, cols].astype(jnp.float32) * do_buf[:, cols].astype(jnp.float32)
            high = prod.astype(jnp.bfloat16)
            low = (prod - high.astype(jnp.float32)).astype(jnp.bfloat16)
            delta = lax.dot_general(ones, high, NT, preferred_element_type=jnp.float32)
            delta += lax.dot_general(ones, low, NT, preferred_element_type=jnp.float32)
            aux[g, h : h + 1, :] = lse_ref[n : n + 1, :] * LOG2E
            aux[g, 8 + h : 9 + h, :] = delta[0:1]
    facts = [wires.send(aux.at[A[t]], auxx.at[a], dev(A[t], b)) for t in (1, 3, 2)]
    own_q.append(local(aux.at[a], auxx.at[a], 14))
    for h in range(BEFORE, GROUP):
        send_head(h)

    passed = {}

    def spread(t):
        rows = slot(A[t], b)
        passed[t] = [[wires.send(x.at[rows], x.at[rows], dev(a, B[n])) for x in kvs] for n in (1, 3)]

    for copy in own_kv:
        copy.wait()
    spread(0)
    for t in (1, 3, 2):
        for copy in first[SIDE - t]:
            copy.wait_recv()
        spread(t)
    for copy in own_q + facts:
        copy.wait()
    for m in range(NLOC):
        tok = slice((m % 2) * BLK, (m % 2 + 1) * BLK)
        for h in range(GROUP):
            part = slice(h * BLK, (h + 1) * BLK)
            stats[m, 0:1, part] = auxx[m // 2, h : h + 1, tok]
            stats[m, 1:2, part] = auxx[m // 2, 8 + h : 9 + h, tok]

    order = facts_ref
    ends = doc_ends(order)
    js = [order[(m // 2 * sa + b * sb) * 2 + m % 2] for m in range(NLOC)]
    ranks = [
        sum((js[i] < js[m] if i > m else js[i] <= js[m]).astype(jnp.int32) for i in range(NLOC) if i != m)
        for m in range(NLOC)
    ]
    for m in range(NLOC):
        here = span((m // 2 * sa + b * sb) * 2 + m % 2, BLK)
        nkv[m] = jnp.concatenate([ks[here, :], vs[here, :]], axis=1)
    kinds = [sum(jnp.where(ranks[i] == r, i, 0) for i in range(NLOC)) for r in range(NLOC)]
    for r, m in enumerate(kinds):
        sj[r] = sum(jnp.where(ranks[i] == r, js[i], 0) for i in range(NLOC))
        skv[r * BLK : (r + 1) * BLK, :] = nkv[m]
        facts_r = stats[m]
        for h in range(GROUP):
            sstats[h, :, r * BLK : (r + 1) * BLK] = facts_r[:, h * BLK : (h + 1) * BLK]
    sacc[...] = jnp.zeros_like(sacc)
    iota = lax.broadcasted_iota(jnp.int32, (BLK, BLK), 0)
    kpos = [sj[r] * BLK + iota for r in range(NLOC)]
    qpos = [sj[r] * BLK + lax.broadcasted_iota(jnp.int32, (1, BLK), 1) for r in range(NLOC)]
    qbegin = [doc_start(pos, ends) for pos in qpos]

    second = {}

    def forward(t):
        up, down = passed[t]
        for copy in up if t < 2 else down:
            copy.wait_recv()
        rows = slot(A[t], B[3] if t < 2 else B[1])
        second[t] = [wires.send(x.at[rows], x.at[rows], dev(a, B[1] if t < 2 else B[3])) for x in kvs]

    def head(h, carry):
        for n in range(2):
            for t in (2, 1, 3):
                head_copy(h, n, t).wait_recv()
        for m in range(NLOC):
            half = slice(m % 2 * BLK, (m % 2 + 1) * BLK)
            nq[m] = qs[m // 2, h, half, :]
            ndo[m] = dos[m // 2, h, half, :]
        for r, m in enumerate(kinds):
            sq[r * BLK : (r + 1) * BLK, :] = nq[m]
            sdo[r * BLK : (r + 1) * BLK, :] = ndo[m]
        st = sstats[h]
        work = []
        for m in range(SIDE):
            keys = skv[0 : (m + 1) * PAIR, :]
            wide = slice(m * PAIR, (m + 1) * PAIR)
            q, do = sq[wide, :], sdo[wide, :]
            sc = lax.dot_general(keys[:, 0:HD], q, NT, preferred_element_type=jnp.float32)
            dp = lax.dot_general(keys[:, HD : 2 * HD], do, NT, preferred_element_type=jnp.float32)
            probs, dscores = [], []
            for u in range(2):
                r = 2 * m + u
                part = slice(u * BLK, (u + 1) * BLK)
                masks = [kpos[n] >= qbegin[r] for n in range(2 * m)]
                masks += [(kpos[n] >= qbegin[r]) & (kpos[n] <= qpos[r]) for n in (2 * m, 2 * m + 1)]
                tok = slice(r * BLK, (r + 1) * BLK)
                p = jnp.exp2(sc[:, part] * (SCALE * LOG2E) - st[0:1, tok])
                p = jnp.where(jnp.concatenate(masks), p, 0.0)
                d = p * (dp[:, part] - st[1:2, tok])
                probs.append(p.astype(jnp.bfloat16))
                dscores.append(d.astype(jnp.bfloat16))
            work.append((keys, q, do, jnp.concatenate(probs, axis=1), jnp.concatenate(dscores, axis=1)))
        for m, (keys, q, do, p, d) in enumerate(work):
            gv = jnp.dot(p, do, preferred_element_type=jnp.float32)
            gk = jnp.dot(d, q, preferred_element_type=jnp.float32)
            for r in range(2 * m + 2):
                rows = slice(r * BLK, (r + 1) * BLK)
                sacc[r, :, HD : 2 * HD] += gv[rows]
                sacc[r, :, 0:HD] += gk[rows]
            g = lax.dot_general(keys[:, 0:HD], d, TN, preferred_element_type=jnp.float32)
            for u in range(2):
                sdq[2 * m + u, h] = g[:, u * BLK : (u + 1) * BLK]
        return carry

    done = 0
    for t, upto in zip((0, 3, 1, 2), AT):
        if upto > done:
            lax.fori_loop(done, upto, head, 0)
            done = upto
        forward(t)
    lax.fori_loop(done, GROUP, head, 0)
    for m in range(NLOC):
        lkv[m] = sacc[ranks[m]]
        mine_dq = sdq[ranks[m]]
        for h in range(GROUP):
            ldq[h][m] = mine_dq[h]

    for t in range(SIDE):
        for copy in passed[t][1 if t < 2 else 0]:
            copy.wait_recv()
        for copy in second[t]:
            copy.wait()
        for copy in passed[t][0] + passed[t][1]:
            copy.wait_send()
    for t in (1, 3, 2):
        for copy in first[t]:
            copy.wait_send()
    for h in range(GROUP):
        for n in range(2):
            for t in (1, 2, 3):
                head_copy(h, n, t).wait_send()


def attend_kernel(order, ks, vs, qs, dos, stats, acc, dqt, inverse, far, jq, iq, ik, iodd, kodd):
    a, b, sa, sb = place()
    core = lax.rem(lax.axis_index("island"), 2)
    ends = doc_ends(order)

    for n in range(NBLK):
        x, y = n // 2 % SIDE, n // 2 // SIDE
        inverse[order[n]] = n
        far[order[n]] = (y + core * (x - y) != b).astype(jnp.int32)
    def plan(i, carry):
        p, odd = carry
        acc[span(i, TOKENS // NLOC), :] = jnp.zeros((TOKENS // NLOC, 2 * HD), jnp.float32)
        dqt[i] = jnp.zeros((HD, QW), jnp.float32)
        j = order[(i // 2 * sa + b * sb) * 2 + lax.rem(i, 2)]
        jq[i] = j
        low = doc_start(j * BLK, ends) // BLK

        q = p
        for n in range(1, MOST // BLK + 1):
            c = jnp.maximum(j - n, 0)
            ik[q] = c
            q = q + jnp.where(j - n >= low, far[c], 0)
        rest = lax.rem(q, 2)
        iodd[odd] = i
        kodd[odd] = ik[jnp.maximum(q - 1, 0)]
        q = q - rest

        def name(t, carry):
            iq[t] = i
            return carry

        lax.fori_loop(p // 2, q // 2, name, 0)
        return q, odd + rest

    total, odd = lax.fori_loop(0, NLOC, plan, (0, 0))
    total = total // 2

    def front(t, size):
        i = iq[t] if size == 2 else iodd[t]
        c = [ik[2 * t + u] for u in range(2)] if size == 2 else [kodd[t]]
        at = [span(inverse[n], BLK) for n in c]
        keys = jnp.concatenate([ks[n, :] for n in at])
        values = jnp.concatenate([vs[n, :] for n in at])
        q = qs[i // 2, :, span(lax.rem(i, 2), BLK), :].reshape(QW, HD)
        do = dos[i // 2, :, span(lax.rem(i, 2), BLK), :].reshape(QW, HD)
        st = stats[i]
        pos = jq[i] * BLK + lax.broadcasted_iota(jnp.int32, (1, BLK), 1)
        iota = lax.broadcasted_iota(jnp.int32, (BLK, BLK), 0)
        mask = jnp.concatenate([n * BLK + iota for n in c]) >= doc_start(pos, ends)
        p, d = weigh(keys, values, q, do, st[0:1], st[1:2], mask)
        return i, at, keys, q, do, p, d

    def back(i, at, keys, q, do, p, d):
        gv = jnp.dot(p, do, preferred_element_type=jnp.float32)
        gk = jnp.dot(d, q, preferred_element_type=jnp.float32)
        for n in range(len(at)):
            acc[at[n], HD : 2 * HD] += gv[n * BLK : (n + 1) * BLK]
            acc[at[n], 0:HD] += gk[n * BLK : (n + 1) * BLK]
        dqt[i] += lax.dot_general(keys, d, TN, preferred_element_type=jnp.float32)

    def group(first, count, size):
        held = front(first, size)
        for u in range(1, count):
            following = front(first + u, size)
            back(*held)
            held = following
        back(*held)

    def run(total, deep, size):
        def many(s, carry):
            group(s * deep, deep, size)
            return carry

        def single(s, carry):
            group(s, 1, size)
            return carry

        lax.fori_loop(0, total // deep, many, 0)
        lax.fori_loop(total // deep * deep, total, single, 0)

    run(total, DEEP, 2)
    run(odd, 3, 1)


def scatter_kernel(
    acc, dqt, lkv, l0, l1, l2, l3, l4, dq, dk, dv, sent, mid, thr, got, grads, dqs, ssem, rsem, lsem
):
    a, b, sa, sb = place()
    A = [lax.rem(a + t, SIDE) for t in range(SIDE)]
    B = [lax.rem(b + t, SIDE) for t in range(SIDE)]

    def dev(aa, bb):
        return {"seq": aa * sa + bb * sb}

    up, down = dev(a, B[1]), dev(a, B[3])
    toward = (up, up, down, down)
    other = (down, down, up, up)
    next_b = (B[1], B[1], B[3], B[3])
    other_b = (B[3], B[3], B[1], B[1])

    def rows_of(bb, t, u):
        return acc[pl.ds(pl.multiple_of((A[t] * sa + bb * sb) * ROWS + u * BLK, BLK), BLK), :]

    order = [(t, u) for ts in ((2, 1), (3, 0)) for u in range(2) for t in ts]
    for t, u in order:
        sent[0, t, u] = rows_of(B[2], t, u).astype(jnp.bfloat16)
    greet([dev(A[1], b), dev(A[3], b), dev(A[2], b), up, down])
    wires = Wires(ssem, rsem)
    through, plain, summed = {}, {}, {}
    for t, u in order:
        through[t, u] = wires.send(sent.at[0, t, u], thr.at[t, u], toward[t])
    for t, u in order:
        sent[1, t, u] = rows_of(other_b[t], t, u).astype(jnp.bfloat16)
        plain[t, u] = wires.send(sent.at[1, t, u], got.at[1 if t < 2 else 0, t, u], other[t])

    heads, copies, last = [], [], []

    def give(t):
        for u in range(2):
            m = 2 * A[t] + u
            for h in range(GROUP):
                part = slice(h * BLK, (h + 1) * BLK)
                g = (dqt[m, :, part] + (l0, l1, l2, l3, l4)[h][m]) * SCALE
                dqs[t, u, :, part] = g.T.astype(jnp.bfloat16)
            dst = dq.at[pl.ds(u * BLK, BLK), span(a, QW)]
            if t:
                heads.append(wires.send(dqs.at[t, u], dst, dev(A[t], b)))
            else:
                copies.append(pltpu.make_async_copy(dqs.at[t, u], dst, lsem.at[u]))
                copies[-1].start()

    def pass_on(t, u):
        through[t, u].wait_recv()
        total = rows_of(next_b[t], t, u) + thr[t, u].astype(jnp.float32)
        mid[t, u] = total.astype(jnp.bfloat16)
        summed[t, u] = wires.send(mid.at[t, u], got.at[0 if t < 2 else 1, t, u], toward[t])

    give(2)
    give(1)
    give(3)
    for t, u in order[:4]:
        pass_on(t, u)
    for t, u in order[4:]:
        pass_on(t, u)
    give(0)
    for t, u in order:
        plain[t, u].wait_recv()
        summed[t, u].wait_recv()
        total = lkv[2 * A[t] + u] + got[0, t, u].astype(jnp.float32) + got[1, t, u].astype(jnp.float32)
        grads[t, u, :, 0:HD] = (total[:, 0:HD] * SCALE).astype(jnp.bfloat16)
        grads[t, u, :, HD : 2 * HD] = total[:, HD : 2 * HD].astype(jnp.bfloat16)
        for n, d in enumerate((dk, dv)):
            src = grads.at[t, u, :, pl.ds(n * HD, HD)]
            dst = d.at[pl.ds(u * BLK, BLK), span(a, HD)]
            if t:
                last.append(wires.send(src, dst, dev(A[t], b)))
            else:
                copies.append(pltpu.make_async_copy(src, dst, lsem.at[2 + 2 * u + n]))
                copies[-1].start()
    for copy in heads + last:
        copy.wait()
    for key in order:
        through[key].wait_send()
        plain[key].wait_send()
        summed[key].wait_send()
    for copy in copies:
        copy.wait()


def emit_kernel(*refs):
    sems = refs[-1]
    copies = [pltpu.make_async_copy(refs[n], refs[n + 3], sems.at[n]) for n in range(3)]
    for copy in copies:
        copy.start()
    for copy in copies:
        copy.wait()


ANY = pl.BlockSpec(memory_space=pl.ANY)
HBM = pl.BlockSpec(memory_space=pltpu.HBM)
VMEM = pl.BlockSpec(memory_space=pltpu.VMEM)
SMEM = pl.BlockSpec(memory_space=pltpu.SMEM)
BF = jnp.bfloat16
F32 = jnp.float32
MIB = 2**20


def shapes(*pairs):
    return [jax.ShapeDtypeStruct(s, d) for s, d in pairs]


def gather_call(facts, query, kv, attn_out, out_grad, log_sums):
    packed = (SIDE, GROUP, ROWS, HD)
    return pl.pallas_call(
        gather_kernel,
        out_shape=shapes(
            ((TOKENS, HD), BF), ((TOKENS, HD), BF), (packed, BF), (packed, BF), ((NLOC, 8, QW), F32),
            ((NLOC, BLK, 2 * HD), F32), *[((NLOC, HD, BLK), F32)] * GROUP,
        ),
        in_specs=[SMEM] + [HBM] * 4 + [VMEM],
        out_specs=[VMEM] * 11,
        scratch_shapes=[
            pltpu.VMEM((ROWS, SIDE * QW), BF),
            pltpu.VMEM((ROWS, SIDE * QW), BF),
            pltpu.VMEM((SIDE, 16, ROWS), F32),
            pltpu.VMEM((SIDE, 16, ROWS), F32),
            pltpu.VMEM((NLOC, BLK, HD), BF),
            pltpu.VMEM((NLOC, BLK, HD), BF),
            pltpu.VMEM((NLOC, BLK, 2 * HD), BF),
            pltpu.VMEM((NLOC * BLK, HD), BF),
            pltpu.VMEM((NLOC * BLK, HD), BF),
            pltpu.VMEM((NLOC * BLK, 2 * HD), BF),
            pltpu.VMEM((GROUP, 8, NLOC * BLK), F32),
            pltpu.VMEM((NLOC, BLK, 2 * HD), F32),
            pltpu.VMEM((NLOC, GROUP, HD, BLK), F32),
            pltpu.SMEM((NLOC,), jnp.int32),
            pltpu.SemaphoreType.DMA((40,)),
            pltpu.SemaphoreType.DMA((40,)),
            pltpu.SemaphoreType.DMA((30,)),
            pltpu.SemaphoreType.DMA((30,)),
            pltpu.SemaphoreType.DMA((16,)),
        ],
        compiler_params=pltpu.CompilerParams(
            collective_id=1, has_side_effects=True, vmem_limit_bytes=45 * MIB
        ),
        name="gather",
    )(facts, query, kv, attn_out, out_grad, log_sums)


def attend_call(facts, ks, vs, qs, dos, stats):
    return pl.pallas_call(
        attend_kernel,
        out_shape=shapes(((TOKENS, 2 * HD), F32), ((NLOC, HD, QW), F32)),
        in_specs=[SMEM] + [VMEM] * 5,
        out_specs=[VMEM, VMEM],
        scratch_shapes=[
            pltpu.SMEM((NBLK,), jnp.int32),
            pltpu.SMEM((NBLK,), jnp.int32),
            pltpu.SMEM((NLOC,), jnp.int32),
            pltpu.SMEM((128,), jnp.int32),
            pltpu.SMEM((256,), jnp.int32),
            pltpu.SMEM((2 * NLOC,), jnp.int32),
            pltpu.SMEM((2 * NLOC,), jnp.int32),
        ],
        compiler_params=pltpu.CompilerParams(vmem_limit_bytes=28 * MIB),
        name="attend",
    )(facts, ks, vs, qs, dos, stats)


def scatter_call(acc, dqt, lkv, *ldq):
    piece = (SIDE, 2, BLK, 2 * HD)
    return pl.pallas_call(
        scatter_kernel,
        out_shape=shapes(((ROWS, SIDE * QW), BF), ((ROWS, SIDE * HD), BF), ((ROWS, SIDE * HD), BF)),
        in_specs=[VMEM] * 8,
        out_specs=[ANY] * 3,
        scratch_shapes=[
            pltpu.VMEM((2,) + piece, BF),
            pltpu.VMEM(piece, BF),
            pltpu.VMEM(piece, BF),
            pltpu.VMEM((2,) + piece, BF),
            pltpu.VMEM(piece, BF),
            pltpu.VMEM((SIDE, 2, BLK, QW), BF),
            pltpu.SemaphoreType.DMA((48,)),
            pltpu.SemaphoreType.DMA((48,)),
            pltpu.SemaphoreType.DMA((8,)),
        ],
        compiler_params=pltpu.CompilerParams(
            collective_id=2, has_side_effects=True, vmem_limit_bytes=28 * MIB
        ),
        name="scatter",
    )(acc, dqt, lkv, *ldq)


def emit_call(*grads):
    return pl.pallas_call(
        emit_kernel,
        out_shape=shapes(*((g.shape, g.dtype) for g in grads)),
        in_specs=[VMEM] * 3,
        out_specs=[HBM] * 3,
        scratch_shapes=[pltpu.SemaphoreType.DMA((3,))],
        compiler_params=pltpu.CompilerParams(vmem_limit_bytes=4 * MIB),
        name="emit",
    )(*grads)


def body(query, key, value, attn_out, out_grad, log_sums, block_order, doc_lengths):
    facts = jnp.concatenate([block_order, doc_lengths])
    kv = jnp.concatenate([key, value], axis=1)
    ks, vs, qs, dos, stats, lkv, *ldq = gather_call(facts, query, kv, attn_out, out_grad, log_sums)
    acc, dqt = attend_call(facts, ks, vs, qs, dos, stats)
    return emit_call(*scatter_call(acc, dqt, lkv, *ldq))


def solution(mesh):
    rows = P(("island", "seq"), None)
    return jax.shard_map(
        body,
        mesh=mesh,
        in_specs=(rows,) * 5 + (P(None, ("island", "seq")), P("island"), P("island")),
        out_specs=(rows,) * 3,
        check_vma=False,
    )
```

```python
import functools
import math

import jax
import jax.numpy as jnp
from jax import lax
from jax.experimental import pallas as pl
from jax.experimental.pallas import tpu as pltpu
from jax.sharding import PartitionSpec as P

MESH = pl.DeviceIdType.MESH
HD = 128
BLK = 128
SIDE = 4
ROWS = 256
GROUP = 5
QW = GROUP * HD
TOKENS = 4096
MOST = 2048
NBLK = 32
PAIR = 2 * BLK
NLOC = 2 * SIDE
SCALE = 1.0 / math.sqrt(HD)
LOG2E = math.log2(math.e)
DEEP = 4
BEFORE = 1
AT = (1, 2, 3, 4)
NT = (((1,), (1,)), ((), ()))
TN = (((0,), (0,)), ((), ()))


def place():
    core = lax.rem(lax.axis_index("island"), 2)
    seq = lax.axis_index("seq")
    x, y = lax.rem(seq, SIDE), seq // SIDE
    a = x + core * (y - x)
    b = y + core * (x - y)
    return a, b, 1 + 3 * core, SIDE - 3 * core


class Wires:
    def __init__(self, send_sems, recv_sems):
        self.send_sems, self.recv_sems, self.count = send_sems, recv_sems, 0

    def send(self, src, dst, device):
        n = self.count
        self.count += 1
        copy = pltpu.make_async_remote_copy(
            src, dst, self.send_sems.at[n], self.recv_sems.at[n], device_id=device, device_id_type=MESH
        )
        copy.start()
        return copy


def span(start, size):
    return pl.ds(pl.multiple_of(start * size, size), size)


def greet(devices):
    barrier = pltpu.get_barrier_semaphore()
    for device in devices:
        pl.semaphore_signal(barrier, inc=1, device_id=device, device_id_type=MESH)
    pl.semaphore_wait(barrier, len(devices))


def weigh(keys, values, q, do, lse, delta, mask):
    st = lax.dot_general(keys, q, NT, preferred_element_type=jnp.float32)
    dpt = lax.dot_general(values, do, NT, preferred_element_type=jnp.float32)
    probs, dscores = [], []
    for n in range(q.shape[0] // BLK):
        part = slice(n * BLK, (n + 1) * BLK)
        p = jnp.exp2(st[:, part] * (SCALE * LOG2E) - lse[:, part])
        p = jnp.where(mask, p, 0.0)
        d = p * (dpt[:, part] - delta[:, part])
        probs.append(p.astype(jnp.bfloat16))
        dscores.append(d.astype(jnp.bfloat16))
    return jnp.concatenate(probs, axis=1), jnp.concatenate(dscores, axis=1)


def doc_start(pos, ends):
    begin = jnp.zeros_like(pos)
    for e in ends:
        begin = jnp.where(pos >= e, e, begin)
    return begin


def doc_ends(facts):
    e0 = facts[NBLK]
    e1 = e0 + facts[NBLK + 1]
    return e0, e1, e1 + facts[NBLK + 2]


def gather_kernel(
    facts_ref, q_ref, kv_ref, o_ref, do_ref, lse_ref,
    ks, vs, qs, dos, stats, lkv, l0, l1, l2, l3, l4,
    o_buf, do_buf, aux, auxx, nq, ndo, nkv, sq, sdo, skv, sstats, sacc, sdq, sj, ssem, rsem, hssem, hrsem, lsem,
):
    a, b, sa, sb = place()
    A = [lax.rem(a + t, SIDE) for t in range(SIDE)]
    B = [lax.rem(b + t, SIDE) for t in range(SIDE)]

    def dev(aa, bb):
        return {"seq": aa * sa + bb * sb}

    def slot(aa, bb):
        return span(aa * sa + bb * sb, ROWS)

    kvs = (ks, vs)
    ldq = (l0, l1, l2, l3, l4)

    def local(src, dst, n):
        copy = pltpu.make_async_copy(src, dst, lsem.at[n])
        copy.start()
        return copy

    loads = [local(o_ref, o_buf, 0), local(do_ref, do_buf, 1)]
    mine = slot(a, b)
    own_kv = [local(kv_ref.at[:, span(a + SIDE * n, HD)], kvs[n].at[mine], 2 + n) for n in range(2)]
    own_q = []
    for h in range(GROUP):
        for n, (s, d) in enumerate(((q_ref, qs), (do_ref, dos))):
            own_q.append(local(s.at[:, span(a * GROUP + h, HD)], d.at[a, h], 4 + 2 * h + n))
    greet([dev(A[1], b), dev(A[3], b), dev(A[2], b), dev(a, B[1]), dev(a, B[3])])
    wires = Wires(ssem, rsem)
    first = {}
    for t in (1, 3, 2):
        first[t] = [
            wires.send(kv_ref.at[:, span(A[t] + SIDE * n, HD)], kvs[n].at[mine], dev(A[t], b))
            for n in range(2)
        ]
    def head_copy(h, n, t):
        src, dst = ((q_ref, qs), (do_ref, dos))[n]
        sem = (h * 2 + n) * 3 + t - 1
        return pltpu.make_async_remote_copy(
            src.at[:, span(A[t] * GROUP + h, HD)], dst.at[a, h], hssem.at[sem], hrsem.at[sem],
            device_id=dev(A[t], b), device_id_type=MESH,
        )

    def send_head(h):
        for n in range(2):
            for t in (2, 1, 3):
                head_copy(h, n, t).start()

    for h in range(BEFORE):
        send_head(h)

    for load in loads:
        load.wait()
    ones = jnp.ones((8, HD), jnp.bfloat16)
    aux[...] = jnp.zeros_like(aux)
    for g in range(SIDE):
        for h in range(GROUP):
            n = g * GROUP + h
            cols = slice(n * HD, (n + 1) * HD)
            prod = o_buf[:, cols].astype(jnp.float32) * do_buf[:, cols].astype(jnp.float32)
            high = prod.astype(jnp.bfloat16)
            low = (prod - high.astype(jnp.float32)).astype(jnp.bfloat16)
            delta = lax.dot_general(ones, high, NT, preferred_element_type=jnp.float32)
            delta += lax.dot_general(ones, low, NT, preferred_element_type=jnp.float32)
            aux[g, h : h + 1, :] = lse_ref[n : n + 1, :] * LOG2E
            aux[g, 8 + h : 9 + h, :] = delta[0:1]
    facts = [wires.send(aux.at[A[t]], auxx.at[a], dev(A[t], b)) for t in (1, 3, 2)]
    own_q.append(local(aux.at[a], auxx.at[a], 14))
    for h in range(BEFORE, GROUP):
        send_head(h)

    passed = {}

    def spread(t):
        rows = slot(A[t], b)
        passed[t] = [[wires.send(x.at[rows], x.at[rows], dev(a, B[n])) for x in kvs] for n in (1, 3)]

    for copy in own_kv:
        copy.wait()
    spread(0)
    for t in (1, 3, 2):
        for copy in first[SIDE - t]:
            copy.wait_recv()
        spread(t)
    for copy in own_q + facts:
        copy.wait()
    for m in range(NLOC):
        tok = slice((m % 2) * BLK, (m % 2 + 1) * BLK)
        for h in range(GROUP):
            part = slice(h * BLK, (h + 1) * BLK)
            stats[m, 0:1, part] = auxx[m // 2, h : h + 1, tok]
            stats[m, 1:2, part] = auxx[m // 2, 8 + h : 9 + h, tok]

    order = facts_ref
    ends = doc_ends(order)
    js = [order[(m // 2 * sa + b * sb) * 2 + m % 2] for m in range(NLOC)]
    ranks = [
        sum((js[i] < js[m] if i > m else js[i] <= js[m]).astype(jnp.int32) for i in range(NLOC) if i != m)
        for m in range(NLOC)
    ]
    for m in range(NLOC):
        here = span((m // 2 * sa + b * sb) * 2 + m % 2, BLK)
        nkv[m] = jnp.concatenate([ks[here, :], vs[here, :]], axis=1)
    kinds = [sum(jnp.where(ranks[i] == r, i, 0) for i in range(NLOC)) for r in range(NLOC)]
    for r, m in enumerate(kinds):
        sj[r] = sum(jnp.where(ranks[i] == r, js[i], 0) for i in range(NLOC))
        skv[r * BLK : (r + 1) * BLK, :] = nkv[m]
        facts_r = stats[m]
        for h in range(GROUP):
            sstats[h, :, r * BLK : (r + 1) * BLK] = facts_r[:, h * BLK : (h + 1) * BLK]
    sacc[...] = jnp.zeros_like(sacc)
    iota = lax.broadcasted_iota(jnp.int32, (BLK, BLK), 0)
    kpos = [sj[r] * BLK + iota for r in range(NLOC)]
    qpos = [sj[r] * BLK + lax.broadcasted_iota(jnp.int32, (1, BLK), 1) for r in range(NLOC)]
    qbegin = [doc_start(pos, ends) for pos in qpos]

    second = {}

    def forward(t):
        up, down = passed[t]
        for copy in up if t < 2 else down:
            copy.wait_recv()
        rows = slot(A[t], B[3] if t < 2 else B[1])
        second[t] = [wires.send(x.at[rows], x.at[rows], dev(a, B[1] if t < 2 else B[3])) for x in kvs]

    def head(h, carry):
        for n in range(2):
            for t in (2, 1, 3):
                head_copy(h, n, t).wait_recv()
        for m in range(NLOC):
            half = slice(m % 2 * BLK, (m % 2 + 1) * BLK)
            nq[m] = qs[m // 2, h, half, :]
            ndo[m] = dos[m // 2, h, half, :]
        for r, m in enumerate(kinds):
            sq[r * BLK : (r + 1) * BLK, :] = nq[m]
            sdo[r * BLK : (r + 1) * BLK, :] = ndo[m]
        st = sstats[h]
        work = []
        for m in range(SIDE):
            keys = skv[0 : (m + 1) * PAIR, :]
            wide = slice(m * PAIR, (m + 1) * PAIR)
            q, do = sq[wide, :], sdo[wide, :]
            sc = lax.dot_general(keys[:, 0:HD], q, NT, preferred_element_type=jnp.float32)
            dp = lax.dot_general(keys[:, HD : 2 * HD], do, NT, preferred_element_type=jnp.float32)
            probs, dscores = [], []
            for u in range(2):
                r = 2 * m + u
                part = slice(u * BLK, (u + 1) * BLK)
                masks = [kpos[n] >= qbegin[r] for n in range(2 * m)]
                masks += [(kpos[n] >= qbegin[r]) & (kpos[n] <= qpos[r]) for n in (2 * m, 2 * m + 1)]
                tok = slice(r * BLK, (r + 1) * BLK)
                p = jnp.exp2(sc[:, part] * (SCALE * LOG2E) - st[0:1, tok])
                p = jnp.where(jnp.concatenate(masks), p, 0.0)
                d = p * (dp[:, part] - st[1:2, tok])
                probs.append(p.astype(jnp.bfloat16))
                dscores.append(d.astype(jnp.bfloat16))
            work.append((keys, q, do, jnp.concatenate(probs, axis=1), jnp.concatenate(dscores, axis=1)))
        for m, (keys, q, do, p, d) in enumerate(work):
            gv = jnp.dot(p, do, preferred_element_type=jnp.float32)
            gk = jnp.dot(d, q, preferred_element_type=jnp.float32)
            for r in range(2 * m + 2):
                rows = slice(r * BLK, (r + 1) * BLK)
                sacc[r, :, HD : 2 * HD] += gv[rows]
                sacc[r, :, 0:HD] += gk[rows]
            g = lax.dot_general(keys[:, 0:HD], d, TN, preferred_element_type=jnp.float32)
            for u in range(2):
                sdq[2 * m + u, h] = g[:, u * BLK : (u + 1) * BLK]
        return carry

    done = 0
    for t, upto in zip((0, 3, 1, 2), AT):
        if upto > done:
            lax.fori_loop(done, upto, head, 0)
            done = upto
        forward(t)
    lax.fori_loop(done, GROUP, head, 0)
    for m in range(NLOC):
        lkv[m] = sacc[ranks[m]]
        mine_dq = sdq[ranks[m]]
        for h in range(GROUP):
            ldq[h][m] = mine_dq[h]

    for t in range(SIDE):
        for copy in passed[t][1 if t < 2 else 0]:
            copy.wait_recv()
        for copy in second[t]:
            copy.wait()
        for copy in passed[t][0] + passed[t][1]:
            copy.wait_send()
    for t in (1, 3, 2):
        for copy in first[t]:
            copy.wait_send()
    for h in range(GROUP):
        for n in range(2):
            for t in (1, 2, 3):
                head_copy(h, n, t).wait_send()


def attend_kernel(order, ks, vs, qs, dos, stats, acc, dqt, inverse, far, jq, iq, ik, iodd, kodd):
    a, b, sa, sb = place()
    core = lax.rem(lax.axis_index("island"), 2)
    ends = doc_ends(order)

    for n in range(NBLK):
        x, y = n // 2 % SIDE, n // 2 // SIDE
        inverse[order[n]] = n
        far[order[n]] = (y + core * (x - y) != b).astype(jnp.int32)
    def plan(i, carry):
        p, odd = carry
        acc[span(i, TOKENS // NLOC), :] = jnp.zeros((TOKENS // NLOC, 2 * HD), jnp.float32)
        dqt[i] = jnp.zeros((HD, QW), jnp.float32)
        j = order[(i // 2 * sa + b * sb) * 2 + lax.rem(i, 2)]
        jq[i] = j
        low = doc_start(j * BLK, ends) // BLK

        q = p
        for n in range(1, MOST // BLK + 1):
            c = jnp.maximum(j - n, 0)
            ik[q] = c
            q = q + jnp.where(j - n >= low, far[c], 0)
        rest = lax.rem(q, 2)
        iodd[odd] = i
        kodd[odd] = ik[jnp.maximum(q - 1, 0)]
        q = q - rest

        def name(t, carry):
            iq[t] = i
            return carry

        lax.fori_loop(p // 2, q // 2, name, 0)
        return q, odd + rest

    total, odd = lax.fori_loop(0, NLOC, plan, (0, 0))
    total = total // 2

    def front(t, size):
        i = iq[t] if size == 2 else iodd[t]
        c = [ik[2 * t + u] for u in range(2)] if size == 2 else [kodd[t]]
        at = [span(inverse[n], BLK) for n in c]
        keys = jnp.concatenate([ks[n, :] for n in at])
        values = jnp.concatenate([vs[n, :] for n in at])
        q = qs[i // 2, :, span(lax.rem(i, 2), BLK), :].reshape(QW, HD)
        do = dos[i // 2, :, span(lax.rem(i, 2), BLK), :].reshape(QW, HD)
        st = stats[i]
        pos = jq[i] * BLK + lax.broadcasted_iota(jnp.int32, (1, BLK), 1)
        iota = lax.broadcasted_iota(jnp.int32, (BLK, BLK), 0)
        mask = jnp.concatenate([n * BLK + iota for n in c]) >= doc_start(pos, ends)
        p, d = weigh(keys, values, q, do, st[0:1], st[1:2], mask)
        return i, at, keys, q, do, p, d

    def back(i, at, keys, q, do, p, d):
        gv = jnp.dot(p, do, preferred_element_type=jnp.float32)
        gk = jnp.dot(d, q, preferred_element_type=jnp.float32)
        for n in range(len(at)):
            acc[at[n], HD : 2 * HD] += gv[n * BLK : (n + 1) * BLK]
            acc[at[n], 0:HD] += gk[n * BLK : (n + 1) * BLK]
        dqt[i] += lax.dot_general(keys, d, TN, preferred_element_type=jnp.float32)

    def group(first, count, size):
        held = front(first, size)
        for u in range(1, count):
            following = front(first + u, size)
            back(*held)
            held = following
        back(*held)

    def run(total, deep, size):
        def many(s, carry):
            group(s * deep, deep, size)
            return carry

        def single(s, carry):
            group(s, 1, size)
            return carry

        lax.fori_loop(0, total // deep, many, 0)
        lax.fori_loop(total // deep * deep, total, single, 0)

    run(total, DEEP, 2)
    run(odd, 3, 1)


def scatter_kernel(
    acc, dqt, lkv, l0, l1, l2, l3, l4, dq, dk, dv, sent, mid, thr, got, grads, dqs, ssem, rsem, lsem
):
    a, b, sa, sb = place()
    A = [lax.rem(a + t, SIDE) for t in range(SIDE)]
    B = [lax.rem(b + t, SIDE) for t in range(SIDE)]

    def dev(aa, bb):
        return {"seq": aa * sa + bb * sb}

    up, down = dev(a, B[1]), dev(a, B[3])
    toward = (up, up, down, down)
    other = (down, down, up, up)
    next_b = (B[1], B[1], B[3], B[3])
    other_b = (B[3], B[3], B[1], B[1])

    def rows_of(bb, t, u):
        return acc[pl.ds(pl.multiple_of((A[t] * sa + bb * sb) * ROWS + u * BLK, BLK), BLK), :]

    order = [(t, u) for ts in ((2, 1), (3, 0)) for u in range(2) for t in ts]
    for t, u in order:
        sent[0, t, u] = rows_of(B[2], t, u).astype(jnp.bfloat16)
    greet([dev(A[1], b), dev(A[3], b), dev(A[2], b), up, down])
    wires = Wires(ssem, rsem)
    through, plain, summed = {}, {}, {}
    for t, u in order:
        through[t, u] = wires.send(sent.at[0, t, u], thr.at[t, u], toward[t])
    for t, u in order:
        sent[1, t, u] = rows_of(other_b[t], t, u).astype(jnp.bfloat16)
        plain[t, u] = wires.send(sent.at[1, t, u], got.at[1 if t < 2 else 0, t, u], other[t])

    heads, copies, last = [], [], []

    def give(t):
        for u in range(2):
            m = 2 * A[t] + u
            for h in range(GROUP):
                part = slice(h * BLK, (h + 1) * BLK)
                g = (dqt[m, :, part] + (l0, l1, l2, l3, l4)[h][m]) * SCALE
                dqs[t, u, :, part] = g.T.astype(jnp.bfloat16)
            dst = dq.at[pl.ds(u * BLK, BLK), span(a, QW)]
            if t:
                heads.append(wires.send(dqs.at[t, u], dst, dev(A[t], b)))
            else:
                copies.append(pltpu.make_async_copy(dqs.at[t, u], dst, lsem.at[u]))
                copies[-1].start()

    def pass_on(t, u):
        through[t, u].wait_recv()
        total = rows_of(next_b[t], t, u) + thr[t, u].astype(jnp.float32)
        mid[t, u] = total.astype(jnp.bfloat16)
        summed[t, u] = wires.send(mid.at[t, u], got.at[0 if t < 2 else 1, t, u], toward[t])

    give(2)
    give(1)
    give(3)
    for t, u in order[:4]:
        pass_on(t, u)
    for t, u in order[4:]:
        pass_on(t, u)
    for t, u in order:
        plain[t, u].wait_recv()
        summed[t, u].wait_recv()
        total = lkv[2 * A[t] + u] + got[0, t, u].astype(jnp.float32) + got[1, t, u].astype(jnp.float32)
        grads[t, u, :, 0:HD] = (total[:, 0:HD] * SCALE).astype(jnp.bfloat16)
        grads[t, u, :, HD : 2 * HD] = total[:, HD : 2 * HD].astype(jnp.bfloat16)
        for n, d in enumerate((dk, dv)):
            src = grads.at[t, u, :, pl.ds(n * HD, HD)]
            dst = d.at[pl.ds(u * BLK, BLK), span(a, HD)]
            if t:
                last.append(wires.send(src, dst, dev(A[t], b)))
            else:
                copies.append(pltpu.make_async_copy(src, dst, lsem.at[2 + 2 * u + n]))
                copies[-1].start()
    give(0)
    for copy in heads + last:
        copy.wait()
    for key in order:
        through[key].wait_send()
        plain[key].wait_send()
        summed[key].wait_send()
    for copy in copies:
        copy.wait()


def emit_kernel(*refs):
    sems = refs[-1]
    copies = [pltpu.make_async_copy(refs[n], refs[n + 3], sems.at[n]) for n in range(3)]
    for copy in copies:
        copy.start()
    for copy in copies:
        copy.wait()


ANY = pl.BlockSpec(memory_space=pl.ANY)
HBM = pl.BlockSpec(memory_space=pltpu.HBM)
VMEM = pl.BlockSpec(memory_space=pltpu.VMEM)
SMEM = pl.BlockSpec(memory_space=pltpu.SMEM)
BF = jnp.bfloat16
F32 = jnp.float32
MIB = 2**20


def shapes(*pairs):
    return [jax.ShapeDtypeStruct(s, d) for s, d in pairs]


def gather_call(facts, query, kv, attn_out, out_grad, log_sums):
    packed = (SIDE, GROUP, ROWS, HD)
    return pl.pallas_call(
        gather_kernel,
        out_shape=shapes(
            ((TOKENS, HD), BF), ((TOKENS, HD), BF), (packed, BF), (packed, BF), ((NLOC, 8, QW), F32),
            ((NLOC, BLK, 2 * HD), F32), *[((NLOC, HD, BLK), F32)] * GROUP,
        ),
        in_specs=[SMEM] + [HBM] * 4 + [VMEM],
        out_specs=[VMEM] * 11,
        scratch_shapes=[
            pltpu.VMEM((ROWS, SIDE * QW), BF),
            pltpu.VMEM((ROWS, SIDE * QW), BF),
            pltpu.VMEM((SIDE, 16, ROWS), F32),
            pltpu.VMEM((SIDE, 16, ROWS), F32),
            pltpu.VMEM((NLOC, BLK, HD), BF),
            pltpu.VMEM((NLOC, BLK, HD), BF),
            pltpu.VMEM((NLOC, BLK, 2 * HD), BF),
            pltpu.VMEM((NLOC * BLK, HD), BF),
            pltpu.VMEM((NLOC * BLK, HD), BF),
            pltpu.VMEM((NLOC * BLK, 2 * HD), BF),
            pltpu.VMEM((GROUP, 8, NLOC * BLK), F32),
            pltpu.VMEM((NLOC, BLK, 2 * HD), F32),
            pltpu.VMEM((NLOC, GROUP, HD, BLK), F32),
            pltpu.SMEM((NLOC,), jnp.int32),
            pltpu.SemaphoreType.DMA((40,)),
            pltpu.SemaphoreType.DMA((40,)),
            pltpu.SemaphoreType.DMA((30,)),
            pltpu.SemaphoreType.DMA((30,)),
            pltpu.SemaphoreType.DMA((16,)),
        ],
        compiler_params=pltpu.CompilerParams(
            collective_id=1, has_side_effects=True, vmem_limit_bytes=45 * MIB
        ),
        name="gather",
    )(facts, query, kv, attn_out, out_grad, log_sums)


def attend_call(facts, ks, vs, qs, dos, stats):
    return pl.pallas_call(
        attend_kernel,
        out_shape=shapes(((TOKENS, 2 * HD), F32), ((NLOC, HD, QW), F32)),
        in_specs=[SMEM] + [VMEM] * 5,
        out_specs=[VMEM, VMEM],
        scratch_shapes=[
            pltpu.SMEM((NBLK,), jnp.int32),
            pltpu.SMEM((NBLK,), jnp.int32),
            pltpu.SMEM((NLOC,), jnp.int32),
            pltpu.SMEM((128,), jnp.int32),
            pltpu.SMEM((256,), jnp.int32),
            pltpu.SMEM((2 * NLOC,), jnp.int32),
            pltpu.SMEM((2 * NLOC,), jnp.int32),
        ],
        compiler_params=pltpu.CompilerParams(vmem_limit_bytes=28 * MIB),
        name="attend",
    )(facts, ks, vs, qs, dos, stats)


def scatter_call(acc, dqt, lkv, *ldq):
    piece = (SIDE, 2, BLK, 2 * HD)
    return pl.pallas_call(
        scatter_kernel,
        out_shape=shapes(((ROWS, SIDE * QW), BF), ((ROWS, SIDE * HD), BF), ((ROWS, SIDE * HD), BF)),
        in_specs=[VMEM] * 8,
        out_specs=[ANY] * 3,
        scratch_shapes=[
            pltpu.VMEM((2,) + piece, BF),
            pltpu.VMEM(piece, BF),
            pltpu.VMEM(piece, BF),
            pltpu.VMEM((2,) + piece, BF),
            pltpu.VMEM(piece, BF),
            pltpu.VMEM((SIDE, 2, BLK, QW), BF),
            pltpu.SemaphoreType.DMA((48,)),
            pltpu.SemaphoreType.DMA((48,)),
            pltpu.SemaphoreType.DMA((8,)),
        ],
        compiler_params=pltpu.CompilerParams(
            collective_id=2, has_side_effects=True, vmem_limit_bytes=28 * MIB
        ),
        name="scatter",
    )(acc, dqt, lkv, *ldq)


def emit_call(*grads):
    return pl.pallas_call(
        emit_kernel,
        out_shape=shapes(*((g.shape, g.dtype) for g in grads)),
        in_specs=[VMEM] * 3,
        out_specs=[HBM] * 3,
        scratch_shapes=[pltpu.SemaphoreType.DMA((3,))],
        compiler_params=pltpu.CompilerParams(vmem_limit_bytes=4 * MIB),
        name="emit",
    )(*grads)


def body(query, key, value, attn_out, out_grad, log_sums, block_order, doc_lengths):
    facts = jnp.concatenate([block_order, doc_lengths])
    kv = jnp.concatenate([key, value], axis=1)
    ks, vs, qs, dos, stats, lkv, *ldq = gather_call(facts, query, kv, attn_out, out_grad, log_sums)
    acc, dqt = attend_call(facts, ks, vs, qs, dos, stats)
    return emit_call(*scatter_call(acc, dqt, lkv, *ldq))


def solution(mesh):
    rows = P(("island", "seq"), None)
    return jax.shard_map(
        body,
        mesh=mesh,
        in_specs=(rows,) * 5 + (P(None, ("island", "seq")), P("island"), P("island")),
        out_specs=(rows,) * 3,
        check_vma=False,
    )
```
